32 devices in a mesh: shard: 2 (over core), ctx: 4 (over y, x), tp: 4 (over z).
Axes of the slice: x: 2, y: 2, z: 4, core: 2. Of those that a mesh axis runs over, the one named last changes fastest.
Arguments:
- inputs: bfloat16 [2, 1024, 1024], P('shard', 'ctx', 'tp'), may hold values from -6 to 6
- w_query: bfloat16 [1024, 2048], P('shard', 'tp'), may hold values from -0.1875 to 0.1875
- key_weight: bfloat16 [1024, 1024], P('shard', 'tp'), may hold values from -0.1875 to 0.1875
- value_weight: bfloat16 [1024, 1024], P('shard', 'tp'), may hold values from -0.1875 to 0.1875
- w_out: bfloat16 [2048, 1024], P('tp', 'shard'), may hold values from -3 to 3
- w_gate: bfloat16 [1024, 3072], P('shard', 'tp'), may hold values from -0.1875 to 0.1875
- w_up: bfloat16 [1024, 3072], P('shard', 'tp'), may hold values from -0.1875 to 0.1875
- w_down: bfloat16 [3072, 1024], P('tp', 'shard'), may hold values from -0.109375 to 0.109375
- norm_attn: bfloat16 [1024], P('shard'), may hold values from 0.5 to 1.5
- norm_mlp: bfloat16 [1024], P('shard'), may hold values from 0.5 to 1.5
- gain_query: bfloat16 [128], P('shard'), may hold values from 0.099609375 to 1.8984375
- gain_key: bfloat16 [128], P('shard'), may hold values from 0.099609375 to 1.8984375
- cotangent: bfloat16 [2, 1024, 1024], P('shard', 'ctx', 'tp'), may hold values from -6 to 6
Outputs:
- outputs: bfloat16 [2, 1024, 1024], P('shard', 'ctx', 'tp')
- d_inputs: bfloat16 [2, 1024, 1024], P('shard', 'ctx', 'tp')
- d_query: float32 [1024, 2048], P(('shard', 'ctx'), 'tp')
- d_key: float32 [1024, 1024], P(('shard', 'ctx'), 'tp')
- d_value: float32 [1024, 1024], P(('shard', 'ctx'), 'tp')
- d_out: float32 [2048, 1024], P('tp', ('shard', 'ctx'))
- d_gate: float32 [1024, 3072], P(('shard', 'ctx'), 'tp')
- d_up: float32 [1024, 3072], P(('shard', 'ctx'), 'tp')
- d_down: float32 [3072, 1024], P('tp', ('shard', 'ctx'))
- d_norm_attn: float32 [1024], P(('shard', 'ctx'))
- d_norm_mlp: float32 [1024], P(('shard', 'ctx'))
- d_gain_query: float32 [128], P(('shard', 'ctx'))
- d_gain_key: float32 [128], P(('shard', 'ctx'))
The draws below stay inside these ranges and needn't reach their ends.
All inputs are finite; a program needn't handle non-finite values.
Results may differ from the reference program's by a relative error of at most 0.025.
Values may be sent and summed in bfloat16 or wider, within the bound.
A program may use at most 128 MiB of HBM per device.

```python
import jax
import jax.numpy as jnp
from jax import lax

MODEL_WIDTH = 1024
QUERY_HEADS = 16
KEY_VALUE_HEADS = 8
HEAD_SIZE = 128
FF = 3072
SEQS = 2
LEN = 1024


def shard_levels(own_key, shape, cuts, smallest, top_value):
    gain, own = 1.0, jax.random.fold_in(own_key, 6)
    for position, blocks in cuts:
        draws = jnp.exp(jax.random.uniform(jax.random.fold_in(own, position), (blocks,), jnp.float32, smallest / len(cuts), top_value / len(cuts)))
        gain = gain * jnp.repeat(draws, shape[position] // blocks).reshape([-1 if axis == position else 1 for axis in range(len(shape))])
    return gain


def gaussian(stream_key, extent, scale, reach, cuts=(), kind=jnp.bfloat16):
    level = shard_levels(stream_key, extent, cuts, -0.22, 0.18) if cuts else 1.0
    entries = jax.random.normal(stream_key, extent, jnp.float32) * scale * level
    return jnp.minimum(jnp.maximum(entries, -reach), reach).astype(kind)


def setup_inputs(seed: int = 0) -> dict:
    streams_of = jax.random.split(jax.random.key(seed), 14)
    inputs = gaussian(streams_of[0], (SEQS, LEN, MODEL_WIDTH), 1.0, 6.0, ((0, 2), (1, 4), (2, 4)))
    w_query = gaussian(streams_of[1], (MODEL_WIDTH, QUERY_HEADS * HEAD_SIZE), MODEL_WIDTH ** -0.5, 0.1875, ((0, 2), (1, 4)))
    key_weight = gaussian(streams_of[2], (MODEL_WIDTH, KEY_VALUE_HEADS * HEAD_SIZE), MODEL_WIDTH ** -0.5, 0.1875, ((0, 2), (1, 4)))
    value_weight = gaussian(streams_of[3], (MODEL_WIDTH, KEY_VALUE_HEADS * HEAD_SIZE), MODEL_WIDTH ** -0.5, 0.1875, ((0, 2), (1, 4)))
    w_out = gaussian(streams_of[4], (QUERY_HEADS * HEAD_SIZE, MODEL_WIDTH), (max(1, 2 * QUERY_HEADS * HEAD_SIZE // LEN)) ** -0.5, 3.0, ((0, 4), (1, 2)))
    w_gate = gaussian(streams_of[5], (MODEL_WIDTH, FF), MODEL_WIDTH ** -0.5, 0.1875, ((0, 2), (1, 4)))
    w_up = gaussian(streams_of[6], (MODEL_WIDTH, FF), MODEL_WIDTH ** -0.5, 0.1875, ((0, 2), (1, 4)))
    w_down = gaussian(streams_of[7], (FF, MODEL_WIDTH), FF ** -0.5, 0.109375, ((0, 4), (1, 2)))
    norm_attn = jnp.clip(1.0 + 0.1 * jax.random.normal(streams_of[8], (MODEL_WIDTH,), jnp.float32), 0.5, 1.5).astype(jnp.bfloat16)
    norm_mlp = jnp.clip(1.0 + 0.1 * jax.random.normal(streams_of[9], (MODEL_WIDTH,), jnp.float32), 0.5, 1.5).astype(jnp.bfloat16)
    gain_query = jnp.clip(1.0 + 0.18 * jax.random.normal(streams_of[10], (HEAD_SIZE,), jnp.float32), 0.099609375, 1.8984375).astype(jnp.bfloat16)
    gain_key = jnp.clip(1.0 + 0.18 * jax.random.normal(streams_of[11], (HEAD_SIZE,), jnp.float32), 0.099609375, 1.8984375).astype(jnp.bfloat16)
    cotangent = gaussian(streams_of[12], (SEQS, LEN, MODEL_WIDTH), 1.0, 6.0, ((0, 2), (1, 4), (2, 4)))
    return dict(inputs=inputs, w_query=w_query, key_weight=key_weight, value_weight=value_weight, w_out=w_out, w_gate=w_gate, w_up=w_up, w_down=w_down, norm_attn=norm_attn, norm_mlp=norm_mlp, gain_query=gain_query, gain_key=gain_key, cotangent=cotangent)


@jax.custom_vjp
def reduced_copy(v):
    return lax.optimization_barrier(v.astype(jnp.bfloat16)).astype(jnp.float32)

@jax.custom_vjp
def reduced_backward(v):
    return v

def low_keep(v):
    return (reduced_copy(v), None)

def low_pass(kept, grad):
    return (grad,)

def back_keep(v):
    return (v, None)

def back_low(kept, grad):
    return (reduced_copy(grad),)
reduced_copy.defvjp(low_keep, low_pass)
reduced_backward.defvjp(back_keep, back_low)
epsilon = 1e-06
rope_base = 1000000.0
masked_score = -1e+30

def matrix_product(first_op, second_op):
    return jnp.dot(first_op, second_op, precision=lax.Precision.HIGHEST, preferred_element_type=jnp.float32)

def rms_norm(value_rows, gain_row):
    return value_rows * lax.rsqrt(lax.optimization_barrier(jnp.mean(value_rows * value_rows, axis=-1, keepdims=True)) + epsilon) * gain_row

def rotary(value_rows, positions):
    half_dim = value_rows.shape[-1] // 2
    frequency = jnp.power(rope_base, -(jnp.arange(half_dim).astype(jnp.float32) * 2.0 / value_rows.shape[-1]))
    angles = positions[:, None] * frequency[None, :]
    cosine = jnp.concatenate([jnp.cos(angles), jnp.cos(angles)], axis=-1)[:, None, :]
    sine_part = jnp.concatenate([jnp.sin(angles), jnp.sin(angles)], axis=-1)[:, None, :]
    turned = jnp.concatenate([-value_rows[..., half_dim:], value_rows[..., :half_dim]], axis=-1)
    return value_rows * cosine + turned * sine_part

def head_block(pieces):
    head_queries, head_keys, head_values = pieces
    token_length = head_keys.shape[0]
    causal = jnp.arange(token_length)[:, None] >= jnp.arange(token_length)[None, :]
    scores = jnp.einsum('gqd,kd->gqk', head_queries, head_keys, precision=lax.Precision.HIGHEST)
    scores = reduced_backward(scores * HEAD_SIZE ** (-0.5))
    scores = jnp.where(causal[None], scores, masked_score)
    row_max = lax.optimization_barrier(jnp.max(scores, axis=-1, keepdims=True))
    exp_scores = jnp.exp(scores - row_max)
    probabilities = reduced_copy(exp_scores / lax.optimization_barrier(jnp.sum(exp_scores, axis=-1, keepdims=True)))
    return jnp.einsum('gqk,kd->gqd', probabilities, head_values, precision=lax.Precision.HIGHEST)

def layer_pass(sequence, params):
    w_query, key_weight, value_weight, w_out, w_gate, w_up, w_down, norm_attn, norm_mlp, gain_query, gain_key = params
    token_length = sequence.shape[0]
    positions = jnp.arange(token_length).astype(jnp.float32)
    normalized_input = reduced_copy(rms_norm(sequence, norm_attn))
    query_rows = reduced_backward(matrix_product(normalized_input, w_query)).reshape(token_length, QUERY_HEADS, HEAD_SIZE)
    key_rows = reduced_backward(matrix_product(normalized_input, key_weight)).reshape(token_length, KEY_VALUE_HEADS, HEAD_SIZE)
    value_rows = reduced_copy(reduced_backward(matrix_product(normalized_input, value_weight))).reshape(token_length, KEY_VALUE_HEADS, HEAD_SIZE)
    query_rows = reduced_copy(rotary(rms_norm(query_rows, gain_query), positions))
    key_rows = reduced_copy(rotary(rms_norm(key_rows, gain_key), positions))
    heads_per_group = QUERY_HEADS // KEY_VALUE_HEADS
    group_shaped = query_rows.reshape(token_length, KEY_VALUE_HEADS, heads_per_group, HEAD_SIZE).transpose(1, 2, 0, 3)
    attended = lax.map(jax.checkpoint(head_block), (group_shaped, key_rows.transpose(1, 0, 2), value_rows.transpose(1, 0, 2)))
    attended = attended.transpose(2, 0, 1, 3).reshape(token_length, QUERY_HEADS * HEAD_SIZE)
    attended = reduced_copy(reduced_backward(attended))
    mixed = sequence + reduced_backward(matrix_product(attended, w_out))
    normed_mlp = reduced_copy(rms_norm(mixed, norm_mlp))
    gate_act = reduced_backward(matrix_product(normed_mlp, w_gate))
    up_act = reduced_backward(matrix_product(normed_mlp, w_up))
    hidden = reduced_copy(jax.nn.silu(gate_act) * up_act)
    return mixed + reduced_backward(matrix_product(hidden, w_down))

def reference(inputs, w_query, key_weight, value_weight, w_out, w_gate, w_up, w_down, norm_attn, norm_mlp, gain_query, gain_key, cotangent):
    params = tuple((array.astype(jnp.float32) for array in (w_query, key_weight, value_weight, w_out, w_gate, w_up, w_down, norm_attn, norm_mlp, gain_query, gain_key)))

    def forward(sequences, weights):
        return lax.map(lambda sequence: layer_pass(sequence, weights), sequences)
    outputs, pullback = jax.vjp(forward, inputs.astype(jnp.float32), params)
    d_inputs, d_params = pullback(cotangent.astype(jnp.float32))
    return (outputs.astype(jnp.bfloat16), d_inputs.astype(jnp.bfloat16), d_params[0], d_params[1], d_params[2], d_params[3], d_params[4], d_params[5], d_params[6], d_params[7], d_params[8], d_params[9], d_params[10])
```

```python
from functools import partial

import jax
import jax.numpy as jnp
from jax import lax
from jax.experimental import pallas as pl
from jax.experimental.pallas import tpu as pltpu
from jax.sharding import PartitionSpec as P

HEAD_SIZE = 128


epsilon = 1e-06
rope_base = 1000000.0
masked_score = -1e30


def rms_norm(value_rows, gain_row):
    return (
        value_rows
        * lax.rsqrt(jnp.mean(value_rows * value_rows, axis=-1, keepdims=True) + epsilon)
        * gain_row
    )


def rms_back(value_rows, gain_row, grad_in):
    factor = lax.rsqrt(jnp.mean(value_rows * value_rows, axis=-1, keepdims=True) + epsilon)
    unit_rows = value_rows * factor
    weighted = grad_in * gain_row
    d_values = factor * (
        weighted - unit_rows * jnp.mean(weighted * unit_rows, axis=-1, keepdims=True)
    )
    return (d_values, jnp.sum(grad_in * unit_rows, axis=0))


def rotary(value_rows, positions):
    half_dim = value_rows.shape[-1] // 2
    frequency = jnp.power(
        rope_base, -(jnp.arange(half_dim).astype(jnp.float32) * 2.0 / value_rows.shape[-1])
    )
    angles = positions[:, None] * frequency[None, :]
    cosine = jnp.concatenate([jnp.cos(angles), jnp.cos(angles)], axis=-1)[:, None, :]
    sine_part = jnp.concatenate([jnp.sin(angles), jnp.sin(angles)], axis=-1)[:, None, :]
    turned = jnp.concatenate([-value_rows[..., half_dim:], value_rows[..., :half_dim]], axis=-1)
    return value_rows * cosine + turned * sine_part


def head_prep(projected, gain_row, positions):
    tokens = projected.shape[0]
    shaped = projected.reshape(tokens, -1, HEAD_SIZE)
    return rotary(rms_norm(shaped, gain_row), positions).reshape(tokens, -1)


def query_block(array, head_index, heads_per_group):
    tokens = array.shape[0]
    piece = array[
        :, head_index * heads_per_group * HEAD_SIZE : (head_index + 1) * heads_per_group * HEAD_SIZE
    ]
    return (
        piece.reshape(tokens, heads_per_group, HEAD_SIZE)
        .transpose(1, 0, 2)
        .reshape(heads_per_group * tokens, HEAD_SIZE)
    )


def block_back(rows_in, heads_per_group):
    tokens = rows_in.shape[0] // heads_per_group
    return (
        rows_in.reshape(heads_per_group, tokens, HEAD_SIZE)
        .transpose(1, 0, 2)
        .reshape(tokens, heads_per_group * HEAD_SIZE)
    )


MESH_IDS = pl.DeviceIdType.MESH


def exchange(name, collective_id, sizes, ops):
    axes = tuple(dict.fromkeys(op[1] for op in ops))
    out_shapes = []
    scratch = []
    total = 0
    for array, axis, kind, dim, rolled in ops:
        n = sizes[axis]
        shape = list(array.shape)
        if kind == "gather":
            shape[dim] *= n
            out_shapes.append(jax.ShapeDtypeStruct(tuple(shape), array.dtype))
        else:
            shape[dim] //= n
            scratch.append(pltpu.VMEM((n, *shape), array.dtype))
            if kind == "scatter":
                out_shapes.append(jax.ShapeDtypeStruct(tuple(shape), jnp.float32))
            else:
                out_shapes.append(jax.ShapeDtypeStruct(array.shape, array.dtype))
        total += array.size
    n_max = max(sizes[a] for a in axes)
    count = len(ops)
    n_scratch = len(scratch)

    def kernel(*refs):
        ins = refs[:count]
        outs = refs[count : 2 * count]
        bufs = list(refs[2 * count : 2 * count + n_scratch])
        send_sem, recv_sem = refs[2 * count + n_scratch :]
        barrier = pltpu.get_barrier_semaphore()
        n_peers = 0
        for axis in axes:
            n = sizes[axis]
            me = lax.axis_index(axis)
            for k in range(1, n):
                pl.semaphore_signal(
                    barrier, inc=1, device_id={axis: lax.rem(me + k, n)}, device_id_type=MESH_IDS
                )
                n_peers += 1
        pl.semaphore_wait(barrier, n_peers)

        def place(ref, index, axis, dim, width, rolled):
            n = sizes[axis]
            if rolled:
                index = lax.rem(index + lax.axis_index("shard") * (n // 2), n)
            start = pl.multiple_of(index * width, width)
            if dim == 0:
                return ref.at[pl.ds(start, width), :]
            return ref.at[:, pl.ds(start, width)]

        sends = []
        first = []
        buf_of = {}
        for i, (array, axis, kind, dim, rolled) in enumerate(ops):
            n = sizes[axis]
            me = lax.axis_index(axis)
            if kind != "gather":
                buf_of[i] = bufs.pop(0)
            for k in range(1, n):
                peer = lax.rem(me + k, n)
                source = lax.rem(me - k + n, n)
                if kind == "gather":
                    width = array.shape[dim]
                    src = ins[i]
                    dst = place(outs[i], me, axis, dim, width, rolled)
                    land = place(outs[i], source, axis, dim, width, rolled)
                else:
                    width = array.shape[dim] // n
                    src = place(ins[i], peer, axis, dim, width, rolled)
                    dst = buf_of[i].at[k]
                    land = dst
                make = partial(
                    pltpu.make_async_remote_copy,
                    src_ref=src,
                    send_sem=send_sem.at[0, i, k],
                    recv_sem=recv_sem.at[0, i, k],
                    device_id={axis: peer},
                    device_id_type=MESH_IDS,
                )
                copy = make(dst_ref=dst)
                copy.start()
                sends.append(copy)
                first.append((i, make(dst_ref=land)))
        for i, (array, axis, kind, dim, rolled) in enumerate(ops):
            if kind == "gather":
                me = lax.axis_index(axis)
                place(outs[i], me, axis, dim, array.shape[dim], rolled)[...] = ins[i][...]
        second = []
        for i, (array, axis, kind, dim, rolled) in enumerate(ops):
            for j, copy in first:
                if i == j:
                    copy.wait_recv()
            if kind == "gather":
                continue
            n = sizes[axis]
            me = lax.axis_index(axis)
            width = array.shape[dim] // n
            summed = place(ins[i], me, axis, dim, width, rolled)[...].astype(jnp.float32)
            for k in range(1, n):
                summed = summed + buf_of[i][k].astype(jnp.float32)
            if kind == "scatter":
                outs[i][...] = summed
                continue
            mine = place(outs[i], me, axis, dim, width, rolled)
            mine[...] = summed.astype(array.dtype)
            for k in range(1, n):
                peer = lax.rem(me + k, n)
                source = lax.rem(me - k + n, n)
                make = partial(
                    pltpu.make_async_remote_copy,
                    src_ref=mine,
                    send_sem=send_sem.at[1, i, k],
                    recv_sem=recv_sem.at[1, i, k],
                    device_id={axis: peer},
                    device_id_type=MESH_IDS,
                )
                copy = make(dst_ref=mine)
                copy.start()
                sends.append(copy)
                second.append(
                    make(dst_ref=place(outs[i], source, axis, dim, width, rolled))
                )
        for copy in second:
            copy.wait_recv()
        for copy in sends:
            copy.wait_send()

    return pl.pallas_call(
        kernel,
        name=name,
        out_shape=tuple(out_shapes),
        in_specs=[pl.BlockSpec(memory_space=pltpu.VMEM)] * count,
        out_specs=tuple([pl.BlockSpec(memory_space=pltpu.VMEM)] * count),
        scratch_shapes=scratch
        + [
            pltpu.SemaphoreType.DMA((2, count, n_max)),
            pltpu.SemaphoreType.DMA((2, count, n_max)),
        ],
        compiler_params=pltpu.CompilerParams(
            collective_id=collective_id, has_side_effects=True, vmem_limit_bytes=24 * 1024 * 1024
        ),
        cost_estimate=pl.CostEstimate(flops=0, bytes_accessed=8 * total, transcendentals=0),
    )(*[op[0] for op in ops])


def total_small(array, sizes):
    axes = ("tp", "ctx", "shard")
    n_max = max(sizes[axis] for axis in axes)

    def kernel(in_ref, out_ref, sent, slots, send_sem, recv_sem):
        barrier = pltpu.get_barrier_semaphore()
        n_peers = 0
        for axis in axes:
            n = sizes[axis]
            me = lax.axis_index(axis)
            for k in range(1, n):
                pl.semaphore_signal(
                    barrier, inc=1, device_id={axis: lax.rem(me + k, n)}, device_id_type=MESH_IDS
                )
                n_peers += 1
        pl.semaphore_wait(barrier, n_peers)
        summed = in_ref[...]
        copies = []
        for stage, axis in enumerate(axes):
            n = sizes[axis]
            me = lax.axis_index(axis)
            sent[stage] = summed
            slots[stage, me] = summed
            here = []
            for k in range(1, n):
                make = partial(
                    pltpu.make_async_remote_copy,
                    src_ref=sent.at[stage],
                    send_sem=send_sem.at[stage, k],
                    recv_sem=recv_sem.at[stage, k],
                    device_id={axis: lax.rem(me + k, n)},
                    device_id_type=MESH_IDS,
                )
                copy = make(dst_ref=slots.at[stage, me])
                copy.start()
                copies.append(copy)
                here.append(make(dst_ref=slots.at[stage, lax.rem(me - k + n, n)]))
            for copy in here:
                copy.wait_recv()
            summed = slots[stage, 0]
            for k in range(1, n):
                summed = summed + slots[stage, k]
        for copy in copies:
            copy.wait_send()
        out_ref[...] = summed

    return pl.pallas_call(
        kernel,
        name="sum_gain_gradients",
        out_shape=jax.ShapeDtypeStruct(array.shape, jnp.float32),
        in_specs=[pl.BlockSpec(memory_space=pltpu.VMEM)],
        out_specs=pl.BlockSpec(memory_space=pltpu.VMEM),
        scratch_shapes=[
            pltpu.VMEM((len(axes), *array.shape), jnp.float32),
            pltpu.VMEM((len(axes), n_max, *array.shape), jnp.float32),
            pltpu.SemaphoreType.DMA((len(axes), n_max)),
            pltpu.SemaphoreType.DMA((len(axes), n_max)),
        ],
        compiler_params=pltpu.CompilerParams(collective_id=6, has_side_effects=True),
    )(array)


def partner(array):
    return lax.ppermute(array, "shard", [(0, 1), (1, 0)])


def grad_shard(grad, dim, n_ctx):
    half = grad.shape[dim] // 2
    low = grad.astype(jnp.bfloat16)
    own = lax.slice_in_dim(low, 0, half, axis=dim)
    theirs = partner(lax.slice_in_dim(low, half, 2 * half, axis=dim))
    both = (own.astype(jnp.float32) + theirs.astype(jnp.float32)).astype(jnp.bfloat16)
    width = half // n_ctx
    me = lax.axis_index("ctx")
    total = lax.dynamic_slice_in_dim(both, me * width, width, dim).astype(jnp.float32)
    for k in range(1, n_ctx):
        piece = lax.dynamic_slice_in_dim(both, (me ^ k) * width, width, dim)
        came = lax.ppermute(piece, "ctx", [(i, i ^ k) for i in range(n_ctx)])
        total = total + came.astype(jnp.float32)
    return total


def body(
    sizes,
    inputs,
    w_query,
    key_weight,
    value_weight,
    w_out,
    w_gate,
    w_up,
    w_down,
    norm_attn,
    norm_mlp,
    gain_query,
    gain_key,
    cotangent,
):
    n_ctx = sizes["ctx"]
    n_tp = sizes["tp"]
    shard_index = lax.axis_index("shard")
    w_query = jnp.concatenate([w_query, partner(w_query)], axis=0)
    key_weight = jnp.concatenate([key_weight, partner(key_weight)], axis=0)
    value_weight = jnp.concatenate([value_weight, partner(value_weight)], axis=0)
    w_out = jnp.concatenate([w_out, partner(w_out)], axis=1)
    w_gate = jnp.concatenate([w_gate, partner(w_gate)], axis=0)
    w_up = jnp.concatenate([w_up, partner(w_up)], axis=0)
    w_down = jnp.concatenate([w_down, partner(w_down)], axis=1)
    width_half = norm_attn.shape[0]
    packed = jnp.concatenate([norm_attn, norm_mlp, gain_query, gain_key]).reshape(-1, HEAD_SIZE)
    pack_rows = packed.shape[0]
    packed = jnp.pad(packed, ((0, -pack_rows % 16), (0, 0)))
    local_tokens = inputs.shape[1]
    width_part = inputs.shape[2]
    offset = lax.axis_index("ctx") * local_tokens
    query_pos = offset + jnp.arange(local_tokens, dtype=jnp.int32)
    positions = query_pos.astype(jnp.float32)
    full_in, gains = exchange(
        "gather_inputs",
        0,
        sizes,
        [
            (inputs.reshape(local_tokens, width_part), "tp", "gather", 1, True),
            (packed, "shard", "gather", 0, False),
        ],
    )
    gains = gains.reshape(2, -1).astype(jnp.float32)
    own_gains = jnp.where(shard_index == 0, gains[0], gains[1])
    other_gains = jnp.where(shard_index == 0, gains[1], gains[0])
    norm_attn = jnp.concatenate([own_gains[:width_half], other_gains[:width_half]])
    norm_mlp = jnp.concatenate(
        [own_gains[width_half : 2 * width_half], other_gains[width_half : 2 * width_half]]
    )
    small = 2 * width_half
    part = HEAD_SIZE // 2
    gain_query = gains[:, small : small + part].reshape(-1)
    gain_key = gains[:, small + part : small + 2 * part].reshape(-1)
    feature_start = lax.rem(lax.axis_index("tp") + shard_index * (n_tp // 2), n_tp) * width_part
    resid_in = full_in.astype(jnp.float32)
    normed_low = rms_norm(resid_in, norm_attn).astype(jnp.bfloat16)
    query_proj = jnp.dot(normed_low, w_query, preferred_element_type=jnp.float32)
    key_proj = jnp.dot(normed_low, key_weight, preferred_element_type=jnp.float32)
    value_proj = jnp.dot(normed_low, value_weight, preferred_element_type=jnp.float32)
    query_pull_fn = partial(head_prep, positions=positions)
    query_heads, query_pull = jax.vjp(query_pull_fn, query_proj, gain_query)
    key_heads, key_pull = jax.vjp(query_pull_fn, key_proj, gain_key)
    query_low = query_heads.astype(jnp.bfloat16)
    key_low = key_heads.astype(jnp.bfloat16)
    value_low = value_proj.astype(jnp.bfloat16)
    key_all, value_all, grad_out = exchange(
        "gather_keys_values",
        1,
        sizes,
        [
            (key_low, "ctx", "gather", 0, False),
            (value_low, "ctx", "gather", 0, False),
            (cotangent.reshape(local_tokens, width_part), "tp", "gather", 1, True),
        ],
    )
    kv_local = key_low.shape[1] // HEAD_SIZE
    heads_per_group = query_low.shape[1] // (HEAD_SIZE * kv_local)
    seq_len = key_all.shape[0]
    key_pos = jnp.arange(seq_len, dtype=jnp.int32)
    causal = jnp.tile(query_pos[:, None] >= key_pos[None, :], (heads_per_group, 1))
    score_scale = HEAD_SIZE ** (-0.5)

    def head_scores(head_index):
        head_rows = query_block(query_low, head_index, heads_per_group)
        head_keys = key_all[:, head_index * HEAD_SIZE : (head_index + 1) * HEAD_SIZE]
        scores = (
            jnp.einsum("qd,kd->qk", head_rows, head_keys, preferred_element_type=jnp.float32)
            * score_scale
        )
        return (head_rows, head_keys, jnp.where(causal, scores, masked_score))

    attended_parts = []
    row_maxima = []
    row_totals = []
    for head_index in range(kv_local):
        head_rows, head_keys, scores = head_scores(head_index)
        row_max = jnp.max(scores, axis=1, keepdims=True)
        exp_scores = jnp.exp(scores - row_max)
        row_total = jnp.sum(exp_scores, axis=1, keepdims=True)
        probs_low = (exp_scores / row_total).astype(jnp.bfloat16)
        head_values = value_all[:, head_index * HEAD_SIZE : (head_index + 1) * HEAD_SIZE]
        head_out = jnp.dot(probs_low, head_values, preferred_element_type=jnp.float32)
        attended_parts.append(block_back(head_out, heads_per_group))
        row_maxima.append(row_max)
        row_totals.append(row_total)
    attended_low = jnp.concatenate(attended_parts, axis=1).astype(jnp.bfloat16)
    attn_part = jnp.dot(attended_low, w_out, preferred_element_type=jnp.float32)
    mixed = resid_in + exchange(
        "sum_attention", 2, sizes, [(attn_part.astype(jnp.bfloat16), "tp", "reduce", 1, True)]
    )[0].astype(jnp.float32)
    normed_mlp_low = rms_norm(mixed, norm_mlp).astype(jnp.bfloat16)
    gate_act = jnp.dot(normed_mlp_low, w_gate, preferred_element_type=jnp.float32)
    up_act = jnp.dot(normed_mlp_low, w_up, preferred_element_type=jnp.float32)
    hidden_low = (jax.nn.silu(gate_act) * up_act).astype(jnp.bfloat16)
    mlp_part = jnp.dot(hidden_low, w_down, preferred_element_type=jnp.float32)
    d_down = jnp.einsum("tf,td->fd", hidden_low, grad_out, preferred_element_type=jnp.float32)
    d_hidden = jnp.einsum("td,fd->tf", grad_out, w_down, preferred_element_type=jnp.float32)
    sigmoid_gate = jax.nn.sigmoid(gate_act)
    d_gate_low = (
        d_hidden * up_act * sigmoid_gate * (1.0 + gate_act * (1.0 - sigmoid_gate))
    ).astype(jnp.bfloat16)
    d_up_low = (d_hidden * gate_act * sigmoid_gate).astype(jnp.bfloat16)
    d_gate = jnp.einsum("td,tf->df", normed_mlp_low, d_gate_low, preferred_element_type=jnp.float32)
    d_up = jnp.einsum("td,tf->df", normed_mlp_low, d_up_low, preferred_element_type=jnp.float32)
    d_normed_mlp = jnp.einsum("tf,df->td", d_gate_low, w_gate, preferred_element_type=jnp.float32)
    d_normed_mlp = d_normed_mlp + jnp.einsum(
        "tf,df->td", d_up_low, w_up, preferred_element_type=jnp.float32
    )
    mlp_sum, d_normed_mlp = exchange(
        "sum_feed_forward",
        3,
        sizes,
        [
            (mlp_part.astype(jnp.bfloat16), "tp", "scatter", 1, True),
            (d_normed_mlp.astype(jnp.bfloat16), "tp", "reduce", 1, True),
        ],
    )
    d_normed_mlp = d_normed_mlp.astype(jnp.float32)
    outputs = (
        (lax.dynamic_slice_in_dim(mixed, feature_start, width_part, 1) + mlp_sum)
        .astype(jnp.bfloat16)
        .reshape(1, local_tokens, width_part)
    )
    d_mix_norm, d_norm_mlp = rms_back(mixed, norm_mlp, d_normed_mlp)
    d_mixed = grad_out.astype(jnp.float32) + d_mix_norm
    d_mixed_low = d_mixed.astype(jnp.bfloat16)
    d_out = jnp.einsum("th,td->hd", attended_low, d_mixed_low, preferred_element_type=jnp.float32)
    d_attended = jnp.einsum(
        "td,hd->th", d_mixed_low, w_out, preferred_element_type=jnp.float32
    ).astype(jnp.bfloat16)
    d_query_parts = []
    d_key_parts = []
    d_value_parts = []
    for head_index in range(kv_local):
        head_rows, head_keys, scores = head_scores(head_index)
        probs_full = jnp.exp(scores - row_maxima[head_index]) / row_totals[head_index]
        probs_low = probs_full.astype(jnp.bfloat16)
        head_values = value_all[:, head_index * HEAD_SIZE : (head_index + 1) * HEAD_SIZE]
        d_rows = query_block(d_attended, head_index, heads_per_group)
        d_probs = jnp.einsum("qd,kd->qk", d_rows, head_values, preferred_element_type=jnp.float32)
        d_value_parts.append(
            jnp.einsum("qk,qd->kd", probs_low, d_rows, preferred_element_type=jnp.float32)
        )
        inner_sum = jnp.sum(probs_full * d_probs, axis=1, keepdims=True)
        d_scores = (probs_full * (d_probs - inner_sum)).astype(jnp.bfloat16)
        d_head_rows = jnp.dot(d_scores, head_keys, preferred_element_type=jnp.float32) * score_scale
        d_query_parts.append(block_back(d_head_rows, heads_per_group))
        d_key_parts.append(
            jnp.einsum("qk,qd->kd", d_scores, head_rows, preferred_element_type=jnp.float32)
            * score_scale
        )
    d_query_heads = jnp.concatenate(d_query_parts, axis=1)
    d_keys_all = jnp.concatenate(d_key_parts, axis=1)
    d_values_all = jnp.concatenate(d_value_parts, axis=1)
    d_key_heads, d_value_proj = exchange(
        "sum_keys_values",
        4,
        sizes,
        [
            (d_keys_all.astype(jnp.bfloat16), "ctx", "scatter", 0, False),
            (d_values_all.astype(jnp.bfloat16), "ctx", "scatter", 0, False),
        ],
    )
    d_query_proj, d_gain_query = query_pull(d_query_heads)
    d_key_proj, d_gain_key = key_pull(d_key_heads)
    d_query_low = d_query_proj.astype(jnp.bfloat16)
    d_key_low = d_key_proj.astype(jnp.bfloat16)
    d_value_low = d_value_proj.astype(jnp.bfloat16)
    d_query = jnp.einsum("td,th->dh", normed_low, d_query_low, preferred_element_type=jnp.float32)
    d_key = jnp.einsum("td,th->dh", normed_low, d_key_low, preferred_element_type=jnp.float32)
    d_value = jnp.einsum("td,th->dh", normed_low, d_value_low, preferred_element_type=jnp.float32)
    d_normed = jnp.einsum("th,dh->td", d_query_low, w_query, preferred_element_type=jnp.float32)
    d_normed = d_normed + jnp.einsum(
        "th,dh->td", d_key_low, key_weight, preferred_element_type=jnp.float32
    )
    d_normed = d_normed + jnp.einsum(
        "th,dh->td", d_value_low, value_weight, preferred_element_type=jnp.float32
    )
    d_normed = exchange(
        "sum_input_gradient", 5, sizes, [(d_normed.astype(jnp.bfloat16), "tp", "reduce", 1, True)]
    )[0].astype(jnp.float32)
    d_in_norm, d_norm_attn = rms_back(resid_in, norm_attn, d_normed)
    d_full = d_mixed + d_in_norm
    d_inputs = (
        lax.dynamic_slice_in_dim(d_full, feature_start, width_part, 1)
        .astype(jnp.bfloat16)
        .reshape(1, local_tokens, width_part)
    )
    norms = jnp.stack([d_norm_attn, d_norm_mlp]).reshape(2, 2, width_half) * (1.0 / n_tp)
    norms = jnp.where(shard_index == 0, norms, norms[:, ::-1]).reshape(-1)
    small = jnp.concatenate([norms, d_gain_query, d_gain_key]).reshape(-1, HEAD_SIZE)
    small = jnp.pad(small, ((0, -small.shape[0] % 8), (0, 0)))
    small = total_small(small, sizes)
    small = small.reshape(-1)
    place = shard_index * n_ctx + lax.axis_index("ctx")
    full_width = 2 * width_half
    ranks = 2 * n_ctx

    def own_part(start, size):
        return lax.dynamic_slice_in_dim(
            small[start : start + size], place * (size // ranks), size // ranks, 0
        )

    gradients = (
        grad_shard(d_query, 0, n_ctx),
        grad_shard(d_key, 0, n_ctx),
        grad_shard(d_value, 0, n_ctx),
        grad_shard(d_out, 1, n_ctx),
        grad_shard(d_gate, 0, n_ctx),
        grad_shard(d_up, 0, n_ctx),
        grad_shard(d_down, 1, n_ctx),
        own_part(0, full_width),
        own_part(full_width, full_width),
        own_part(2 * full_width, HEAD_SIZE),
        own_part(2 * full_width + HEAD_SIZE, HEAD_SIZE),
    )
    return (outputs, d_inputs) + tuple(gradients)


def solution(mesh):
    return jax.shard_map(
        partial(body, dict(mesh.shape)),
        mesh=mesh,
        in_specs=(
            P("shard", "ctx", "tp"),
            P("shard", "tp"),
            P("shard", "tp"),
            P("shard", "tp"),
            P("tp", "shard"),
            P("shard", "tp"),
            P("shard", "tp"),
            P("tp", "shard"),
            P("shard"),
            P("shard"),
            P("shard"),
            P("shard"),
            P("shard", "ctx", "tp"),
        ),
        out_specs=(
            P("shard", "ctx", "tp"),
            P("shard", "ctx", "tp"),
            P(("shard", "ctx"), "tp"),
            P(("shard", "ctx"), "tp"),
            P(("shard", "ctx"), "tp"),
            P("tp", ("shard", "ctx")),
            P(("shard", "ctx"), "tp"),
            P(("shard", "ctx"), "tp"),
            P("tp", ("shard", "ctx")),
            P(("shard", "ctx")),
            P(("shard", "ctx")),
            P(("shard", "ctx")),
            P(("shard", "ctx")),
        ),
        check_vma=False,
    )
```

```python
from functools import partial

import jax
import jax.numpy as jnp
from jax import lax
from jax.experimental import pallas as pl
from jax.experimental.pallas import tpu as pltpu
from jax.sharding import PartitionSpec as P

HEAD_SIZE = 128


epsilon = 1e-06
rope_base = 1000000.0
masked_score = -1e30


def rms_norm(value_rows, gain_row):
    return (
        value_rows
        * lax.rsqrt(jnp.mean(value_rows * value_rows, axis=-1, keepdims=True) + epsilon)
        * gain_row
    )


def rms_back(value_rows, gain_row, grad_in):
    factor = lax.rsqrt(jnp.mean(value_rows * value_rows, axis=-1, keepdims=True) + epsilon)
    unit_rows = value_rows * factor
    weighted = grad_in * gain_row
    d_values = factor * (
        weighted - unit_rows * jnp.mean(weighted * unit_rows, axis=-1, keepdims=True)
    )
    return (d_values, jnp.sum(grad_in * unit_rows, axis=0))


def rotary(value_rows, positions):
    half_dim = value_rows.shape[-1] // 2
    frequency = jnp.power(
        rope_base, -(jnp.arange(half_dim).astype(jnp.float32) * 2.0 / value_rows.shape[-1])
    )
    angles = positions[:, None] * frequency[None, :]
    cosine = jnp.concatenate([jnp.cos(angles), jnp.cos(angles)], axis=-1)[:, None, :]
    sine_part = jnp.concatenate([jnp.sin(angles), jnp.sin(angles)], axis=-1)[:, None, :]
    turned = jnp.concatenate([-value_rows[..., half_dim:], value_rows[..., :half_dim]], axis=-1)
    return value_rows * cosine + turned * sine_part


def head_prep(projected, gain_row, positions):
    tokens = projected.shape[0]
    shaped = projected.reshape(tokens, -1, HEAD_SIZE)
    return rotary(rms_norm(shaped, gain_row), positions).reshape(tokens, -1)


def query_block(array, head_index, heads_per_group):
    tokens = array.shape[0]
    piece = array[
        :, head_index * heads_per_group * HEAD_SIZE : (head_index + 1) * heads_per_group * HEAD_SIZE
    ]
    return (
        piece.reshape(tokens, heads_per_group, HEAD_SIZE)
        .transpose(1, 0, 2)
        .reshape(heads_per_group * tokens, HEAD_SIZE)
    )


def block_back(rows_in, heads_per_group):
    tokens = rows_in.shape[0] // heads_per_group
    return (
        rows_in.reshape(heads_per_group, tokens, HEAD_SIZE)
        .transpose(1, 0, 2)
        .reshape(tokens, heads_per_group * HEAD_SIZE)
    )


MESH_IDS = pl.DeviceIdType.MESH


def exchange(name, collective_id, sizes, ops):
    axes = []
    out_shapes = []
    scratch = []
    slots_of = []
    total = 0
    n_sems = 0
    for array, op_axes, kind, dim in ops:
        axes += op_axes
        shape = list(array.shape)
        slots_of.append(len(scratch))
        total += array.size
        n = sizes[op_axes[0]]
        dtype = array.dtype
        if kind == "gather":
            shape[dim] *= n
            n_sems += n
        elif kind == "scatter":
            shape[dim] //= n
            scratch.append(pltpu.VMEM((n, *shape), dtype))
            dtype = jnp.float32
            n_sems += n
        elif kind == "reduce":
            scratch.append(pltpu.VMEM((n, shape[0], shape[1] // n), dtype))
            n_sems += 2 * n
        elif kind == "grad":
            half = shape[0] // 2
            scratch.append(pltpu.VMEM((half, shape[1]), dtype))
            scratch.append(pltpu.VMEM((half, shape[1]), dtype))
            shape[0] = half // sizes["ctx"]
            scratch.append(pltpu.VMEM((sizes["ctx"], *shape), dtype))
            dtype = jnp.float32
            n_sems += 1 + sizes["ctx"]
        else:
            n_max = max(sizes[axis] for axis in op_axes)
            scratch.append(pltpu.VMEM((len(op_axes), *shape), dtype))
            scratch.append(pltpu.VMEM((len(op_axes), n_max, *shape), dtype))
            n_sems += sum(sizes[axis] for axis in op_axes)
        out_shapes.append(jax.ShapeDtypeStruct(tuple(shape), dtype))
    axes = tuple(dict.fromkeys(axes))
    count = len(ops)

    def kernel(*refs):
        ins = refs[:count]
        outs = refs[count : 2 * count]
        bufs = refs[2 * count : -2]
        send_sem, recv_sem = refs[-2:]
        barrier = pltpu.get_barrier_semaphore()
        n_peers = 0
        for axis in axes:
            n = sizes[axis]
            me = lax.axis_index(axis)
            for k in range(1, n):
                pl.semaphore_signal(
                    barrier, inc=1, device_id={axis: lax.rem(me + k, n)}, device_id_type=MESH_IDS
                )
                n_peers += 1
        pl.semaphore_wait(barrier, n_peers)
        sends = []
        used = [0]

        def send(src, dst, land, axis, peer):
            index = used[0]
            used[0] += 1
            make = partial(
                pltpu.make_async_remote_copy,
                src_ref=src,
                send_sem=send_sem.at[index],
                recv_sem=recv_sem.at[index],
                device_id={axis: peer},
                device_id_type=MESH_IDS,
            )
            copy = make(dst_ref=dst)
            copy.start()
            sends.append(copy)
            return make(dst_ref=land)

        def peers(axis):
            n = sizes[axis]
            me = lax.axis_index(axis)
            return [(k, lax.rem(me + k, n), lax.rem(me - k + n, n)) for k in range(1, n)]

        def place(ref, index, axis, dim, width):
            n = sizes[axis]
            if axis == "tp":
                index = lax.rem(index + lax.axis_index("shard") * (n // 2), n)
            start = pl.multiple_of(index * width, width)
            if dim == 0:
                return ref.at[pl.ds(start, width), :]
            return ref.at[:, pl.ds(start, width)]

        def total_send(i, stage, value):
            axis = ops[i][1][stage]
            sent, slots = bufs[slots_of[i] : slots_of[i] + 2]
            me = lax.axis_index(axis)
            sent[stage] = value
            slots[stage, me] = value
            return [
                send(sent.at[stage], slots.at[stage, me], slots.at[stage, source], axis, peer)
                for k, peer, source in peers(axis)
            ]

        def total_take(i, stage, pending):
            slots = bufs[slots_of[i] + 1]
            for copy in pending:
                copy.wait_recv()
            value = slots[stage, 0]
            for k in range(1, sizes[ops[i][1][stage]]):
                value = value + slots[stage, k]
            return value

        pending = {}
        kinds = {
            kind: [i for i in range(count) if ops[i][2] == kind]
            for kind in ("total", "reduce", "scatter", "gather", "grad")
        }
        for i in kinds["total"]:
            pending[i] = total_send(i, 0, ins[i][...])
        for i in kinds["reduce"] + kinds["scatter"]:
            array, (axis,), kind, dim = ops[i]
            width = array.shape[dim] // sizes[axis]
            buf = bufs[slots_of[i]]
            pending[i] = [
                send(place(ins[i], peer, axis, dim, width), buf.at[k], buf.at[k], axis, peer)
                for k, peer, source in peers(axis)
            ]
        for i in kinds["gather"]:
            array, (axis,), kind, dim = ops[i]
            width = array.shape[dim]
            me = lax.axis_index(axis)
            pending[i] = [
                send(
                    ins[i],
                    place(outs[i], me, axis, dim, width),
                    place(outs[i], source, axis, dim, width),
                    axis,
                    peer,
                )
                for k, peer, source in peers(axis)
            ]
        for i in kinds["grad"]:
            half = ops[i][0].shape[0] // 2
            came = bufs[slots_of[i]]
            other = 1 - lax.axis_index("shard")
            pending[i] = [send(ins[i].at[pl.ds(half, half), :], came, came, "shard", other)]
        for i in kinds["gather"]:
            array, (axis,), kind, dim = ops[i]
            me = lax.axis_index(axis)
            place(outs[i], me, axis, dim, array.shape[dim])[...] = ins[i][...]
        for i in kinds["grad"]:
            half = ops[i][0].shape[0] // 2
            came, both, slots = bufs[slots_of[i] : slots_of[i] + 3]
            pending[i][0].wait_recv()
            both[...] = (
                ins[i][pl.ds(0, half), :].astype(jnp.float32) + came[...].astype(jnp.float32)
            ).astype(both.dtype)
            width = half // sizes["ctx"]
            pending[i] = [
                send(place(both, peer, "ctx", 0, width), slots.at[k], slots.at[k], "ctx", peer)
                for k, peer, source in peers("ctx")
            ]
        value = {}
        for i in kinds["total"]:
            value[i] = total_take(i, 0, pending[i])
            if len(ops[i][1]) > 1:
                pending[i] = total_send(i, 1, value[i])
        second = []
        for i in kinds["reduce"] + kinds["scatter"]:
            array, (axis,), kind, dim = ops[i]
            buf = bufs[slots_of[i]]
            me = lax.axis_index(axis)
            width = array.shape[dim] // sizes[axis]
            for copy in pending[i]:
                copy.wait_recv()
            summed = place(ins[i], me, axis, dim, width)[...].astype(jnp.float32)
            for k in range(1, sizes[axis]):
                summed = summed + buf[k].astype(jnp.float32)
            if kind == "scatter":
                outs[i][...] = summed
                continue
            mine = place(outs[i], me, axis, dim, width)
            mine[...] = summed.astype(array.dtype)
            second += [
                send(mine, mine, place(outs[i], source, axis, dim, width), axis, peer)
                for k, peer, source in peers(axis)
            ]
        for i in kinds["total"]:
            for stage in range(1, len(ops[i][1])):
                value[i] = total_take(i, stage, pending[i])
                if stage + 1 < len(ops[i][1]):
                    pending[i] = total_send(i, stage + 1, value[i])
            outs[i][...] = value[i]
        for i in kinds["grad"]:
            both, slots = bufs[slots_of[i] + 1 : slots_of[i] + 3]
            for copy in pending[i]:
                copy.wait_recv()
            width = slots.shape[1]
            summed = place(both, lax.axis_index("ctx"), "ctx", 0, width)[...].astype(jnp.float32)
            for k in range(1, sizes["ctx"]):
                summed = summed + slots[k].astype(jnp.float32)
            outs[i][...] = summed
        for i in kinds["gather"]:
            second += pending[i]
        for copy in second:
            copy.wait_recv()
        for copy in sends:
            copy.wait_send()

    return pl.pallas_call(
        kernel,
        name=name,
        out_shape=tuple(out_shapes),
        in_specs=[pl.BlockSpec(memory_space=pltpu.VMEM)] * count,
        out_specs=tuple([pl.BlockSpec(memory_space=pltpu.VMEM)] * count),
        scratch_shapes=scratch
        + [pltpu.SemaphoreType.DMA((n_sems,)), pltpu.SemaphoreType.DMA((n_sems,))],
        compiler_params=pltpu.CompilerParams(
            collective_id=collective_id, has_side_effects=True, vmem_limit_bytes=32 * 1024 * 1024
        ),
        cost_estimate=pl.CostEstimate(flops=0, bytes_accessed=8 * total, transcendentals=0),
    )(*[op[0] for op in ops])


def partner(array):
    return lax.ppermute(array, "shard", [(0, 1), (1, 0)])


GRAD_AXES = ("shard", "ctx")
ALL_AXES = ("tp", "ctx", "shard")
TP = ("tp",)
CTX = ("ctx",)


def body(
    sizes,
    inputs,
    w_query,
    key_weight,
    value_weight,
    w_out,
    w_gate,
    w_up,
    w_down,
    norm_attn,
    norm_mlp,
    gain_query,
    gain_key,
    cotangent,
):
    n_ctx = sizes["ctx"]
    n_tp = sizes["tp"]
    shard_index = lax.axis_index("shard")
    w_query = jnp.concatenate([w_query, partner(w_query)], axis=0)
    key_weight = jnp.concatenate([key_weight, partner(key_weight)], axis=0)
    value_weight = jnp.concatenate([value_weight, partner(value_weight)], axis=0)
    w_out = jnp.concatenate([w_out, partner(w_out)], axis=1)
    w_gate = jnp.concatenate([w_gate, partner(w_gate)], axis=0)
    w_up = jnp.concatenate([w_up, partner(w_up)], axis=0)
    w_down = jnp.concatenate([w_down, partner(w_down)], axis=1)
    width_half = norm_attn.shape[0]
    packed = jnp.concatenate([norm_attn, norm_mlp, gain_query, gain_key]).reshape(-1, HEAD_SIZE)
    pack_rows = packed.shape[0]
    packed = jnp.pad(packed, ((0, -pack_rows % 16), (0, 0)))
    local_tokens = inputs.shape[1]
    width_part = inputs.shape[2]
    offset = lax.axis_index("ctx") * local_tokens
    query_pos = offset + jnp.arange(local_tokens, dtype=jnp.int32)
    positions = query_pos.astype(jnp.float32)
    full_in, gains = exchange(
        "gather_inputs",
        0,
        sizes,
        [
            (inputs.reshape(local_tokens, width_part), TP, "gather", 1),
            (packed, ("shard",), "gather", 0),
        ],
    )
    gains = gains.reshape(2, -1).astype(jnp.float32)
    own_gains = jnp.where(shard_index == 0, gains[0], gains[1])
    other_gains = jnp.where(shard_index == 0, gains[1], gains[0])
    norm_attn = jnp.concatenate([own_gains[:width_half], other_gains[:width_half]])
    norm_mlp = jnp.concatenate(
        [own_gains[width_half : 2 * width_half], other_gains[width_half : 2 * width_half]]
    )
    small = 2 * width_half
    part = HEAD_SIZE // 2
    gain_query = gains[:, small : small + part].reshape(-1)
    gain_key = gains[:, small + part : small + 2 * part].reshape(-1)
    feature_start = lax.rem(lax.axis_index("tp") + shard_index * (n_tp // 2), n_tp) * width_part
    resid_in = full_in.astype(jnp.float32)
    normed_low = rms_norm(resid_in, norm_attn).astype(jnp.bfloat16)
    query_proj = jnp.dot(normed_low, w_query, preferred_element_type=jnp.float32)
    key_proj = jnp.dot(normed_low, key_weight, preferred_element_type=jnp.float32)
    value_proj = jnp.dot(normed_low, value_weight, preferred_element_type=jnp.float32)
    query_pull_fn = partial(head_prep, positions=positions)
    query_heads, query_pull = jax.vjp(query_pull_fn, query_proj, gain_query)
    key_heads, key_pull = jax.vjp(query_pull_fn, key_proj, gain_key)
    query_low = query_heads.astype(jnp.bfloat16)
    key_low = key_heads.astype(jnp.bfloat16)
    value_low = value_proj.astype(jnp.bfloat16)
    key_all, value_all, grad_out = exchange(
        "gather_keys_values",
        1,
        sizes,
        [
            (key_low, CTX, "gather", 0),
            (value_low, CTX, "gather", 0),
            (cotangent.reshape(local_tokens, width_part), TP, "gather", 1),
        ],
    )
    kv_local = key_low.shape[1] // HEAD_SIZE
    heads_per_group = query_low.shape[1] // (HEAD_SIZE * kv_local)
    seq_len = key_all.shape[0]
    key_pos = jnp.arange(seq_len, dtype=jnp.int32)
    causal = jnp.tile(query_pos[:, None] >= key_pos[None, :], (heads_per_group, 1))
    score_scale = HEAD_SIZE ** (-0.5)

    def head_scores(head_index):
        head_rows = query_block(query_low, head_index, heads_per_group)
        head_keys = key_all[:, head_index * HEAD_SIZE : (head_index + 1) * HEAD_SIZE]
        scores = (
            jnp.einsum("qd,kd->qk", head_rows, head_keys, preferred_element_type=jnp.float32)
            * score_scale
        )
        return (head_rows, head_keys, jnp.where(causal, scores, masked_score))

    attended_parts = []
    row_maxima = []
    row_totals = []
    for head_index in range(kv_local):
        head_rows, head_keys, scores = head_scores(head_index)
        row_max = jnp.max(scores, axis=1, keepdims=True)
        exp_scores = jnp.exp(scores - row_max)
        row_total = jnp.sum(exp_scores, axis=1, keepdims=True)
        probs_low = (exp_scores / row_total).astype(jnp.bfloat16)
        head_values = value_all[:, head_index * HEAD_SIZE : (head_index + 1) * HEAD_SIZE]
        head_out = jnp.dot(probs_low, head_values, preferred_element_type=jnp.float32)
        attended_parts.append(block_back(head_out, heads_per_group))
        row_maxima.append(row_max)
        row_totals.append(row_total)
    attended_low = jnp.concatenate(attended_parts, axis=1).astype(jnp.bfloat16)
    attn_part = jnp.dot(attended_low, w_out, preferred_element_type=jnp.float32)
    mixed = resid_in + exchange(
        "sum_attention", 2, sizes, [(attn_part.astype(jnp.bfloat16), TP, "reduce", 1)]
    )[0].astype(jnp.float32)
    normed_mlp_low = rms_norm(mixed, norm_mlp).astype(jnp.bfloat16)
    gate_act = jnp.dot(normed_mlp_low, w_gate, preferred_element_type=jnp.float32)
    up_act = jnp.dot(normed_mlp_low, w_up, preferred_element_type=jnp.float32)
    hidden_low = (jax.nn.silu(gate_act) * up_act).astype(jnp.bfloat16)
    mlp_part = jnp.dot(hidden_low, w_down, preferred_element_type=jnp.float32)
    d_down = jnp.einsum("tf,td->df", hidden_low, grad_out, preferred_element_type=jnp.float32)
    d_hidden = jnp.einsum("td,fd->tf", grad_out, w_down, preferred_element_type=jnp.float32)
    sigmoid_gate = jax.nn.sigmoid(gate_act)
    d_gate_low = (
        d_hidden * up_act * sigmoid_gate * (1.0 + gate_act * (1.0 - sigmoid_gate))
    ).astype(jnp.bfloat16)
    d_up_low = (d_hidden * gate_act * sigmoid_gate).astype(jnp.bfloat16)
    d_gate = jnp.einsum("td,tf->df", normed_mlp_low, d_gate_low, preferred_element_type=jnp.float32)
    d_up = jnp.einsum("td,tf->df", normed_mlp_low, d_up_low, preferred_element_type=jnp.float32)
    d_normed_mlp = jnp.einsum("tf,df->td", d_gate_low, w_gate, preferred_element_type=jnp.float32)
    d_normed_mlp = d_normed_mlp + jnp.einsum(
        "tf,df->td", d_up_low, w_up, preferred_element_type=jnp.float32
    )
    d_normed_mlp, d_down, d_gate, d_up = exchange(
        "sum_feed_forward",
        3,
        sizes,
        [
            (d_normed_mlp.astype(jnp.bfloat16), TP, "reduce", 1),
            (d_down.astype(jnp.bfloat16), GRAD_AXES, "grad", 0),
            (d_gate.astype(jnp.bfloat16), GRAD_AXES, "grad", 0),
            (d_up.astype(jnp.bfloat16), GRAD_AXES, "grad", 0),
        ],
    )
    d_normed_mlp = d_normed_mlp.astype(jnp.float32)
    d_mix_norm, d_norm_mlp = rms_back(mixed, norm_mlp, d_normed_mlp)
    d_mixed = grad_out.astype(jnp.float32) + d_mix_norm
    d_mixed_low = d_mixed.astype(jnp.bfloat16)
    d_out = jnp.einsum("th,td->dh", attended_low, d_mixed_low, preferred_element_type=jnp.float32)
    d_attended = jnp.einsum(
        "td,hd->th", d_mixed_low, w_out, preferred_element_type=jnp.float32
    ).astype(jnp.bfloat16)
    d_query_parts = []
    d_key_parts = []
    d_value_parts = []
    for head_index in range(kv_local):
        head_rows, head_keys, scores = head_scores(head_index)
        probs_full = jnp.exp(scores - row_maxima[head_index]) / row_totals[head_index]
        probs_low = probs_full.astype(jnp.bfloat16)
        head_values = value_all[:, head_index * HEAD_SIZE : (head_index + 1) * HEAD_SIZE]
        d_rows = query_block(d_attended, head_index, heads_per_group)
        d_probs = jnp.einsum("qd,kd->qk", d_rows, head_values, preferred_element_type=jnp.float32)
        d_value_parts.append(
            jnp.einsum("qk,qd->kd", probs_low, d_rows, preferred_element_type=jnp.float32)
        )
        inner_sum = jnp.sum(probs_full * d_probs, axis=1, keepdims=True)
        d_scores = (probs_full * (d_probs - inner_sum)).astype(jnp.bfloat16)
        d_head_rows = jnp.dot(d_scores, head_keys, preferred_element_type=jnp.float32) * score_scale
        d_query_parts.append(block_back(d_head_rows, heads_per_group))
        d_key_parts.append(
            jnp.einsum("qk,qd->kd", d_scores, head_rows, preferred_element_type=jnp.float32)
            * score_scale
        )
    d_query_heads = jnp.concatenate(d_query_parts, axis=1)
    d_keys_all = jnp.concatenate(d_key_parts, axis=1)
    d_values_all = jnp.concatenate(d_value_parts, axis=1)
    d_key_heads, d_value_proj, mlp_sum = exchange(
        "sum_keys_values",
        4,
        sizes,
        [
            (d_keys_all.astype(jnp.bfloat16), CTX, "scatter", 0),
            (d_values_all.astype(jnp.bfloat16), CTX, "scatter", 0),
            (mlp_part.astype(jnp.bfloat16), TP, "scatter", 1),
        ],
    )
    outputs = (
        (lax.dynamic_slice_in_dim(mixed, feature_start, width_part, 1) + mlp_sum)
        .astype(jnp.bfloat16)
        .reshape(1, local_tokens, width_part)
    )
    d_query_proj, d_gain_query = query_pull(d_query_heads)
    d_key_proj, d_gain_key = key_pull(d_key_heads)
    d_query_low = d_query_proj.astype(jnp.bfloat16)
    d_key_low = d_key_proj.astype(jnp.bfloat16)
    d_value_low = d_value_proj.astype(jnp.bfloat16)
    d_query = jnp.einsum("td,th->dh", normed_low, d_query_low, preferred_element_type=jnp.float32)
    d_key = jnp.einsum("td,th->dh", normed_low, d_key_low, preferred_element_type=jnp.float32)
    d_value = jnp.einsum("td,th->dh", normed_low, d_value_low, preferred_element_type=jnp.float32)
    d_normed = jnp.einsum("th,dh->td", d_query_low, w_query, preferred_element_type=jnp.float32)
    d_normed = d_normed + jnp.einsum(
        "th,dh->td", d_key_low, key_weight, preferred_element_type=jnp.float32
    )
    d_normed = d_normed + jnp.einsum(
        "th,dh->td", d_value_low, value_weight, preferred_element_type=jnp.float32
    )
    factor = lax.rsqrt(jnp.mean(resid_in * resid_in, axis=-1, keepdims=True) + epsilon)
    unit_rows = resid_in * factor
    weighed = d_normed * unit_rows
    d_norm_attn = jnp.sum(weighed, axis=0)
    row_part = jnp.sum(weighed * norm_attn, axis=-1).reshape(-1, 128)
    stat_rows = row_part.shape[0]
    row_part = jnp.pad(row_part, ((0, -stat_rows % 8), (0, 0)))
    norms = jnp.stack([d_norm_attn, d_norm_mlp * (1.0 / n_tp)]).reshape(2, 2, width_half)
    norms = jnp.where(shard_index == 0, norms, norms[:, ::-1]).reshape(-1)
    small = jnp.concatenate([norms, d_gain_query, d_gain_key]).reshape(-1, HEAD_SIZE)
    small = jnp.pad(small, ((0, -small.shape[0] % 8), (0, 0)))
    row_sum, small, d_normed, d_out, d_query, d_key, d_value = exchange(
        "sum_input_gradient",
        5,
        sizes,
        [
            (row_part, TP, "total", 0),
            (small, ALL_AXES, "total", 0),
            (d_normed.astype(jnp.bfloat16), TP, "scatter", 1),
            (d_out.astype(jnp.bfloat16), GRAD_AXES, "grad", 0),
            (d_query.astype(jnp.bfloat16), GRAD_AXES, "grad", 0),
            (d_key.astype(jnp.bfloat16), GRAD_AXES, "grad", 0),
            (d_value.astype(jnp.bfloat16), GRAD_AXES, "grad", 0),
        ],
    )

    def own_columns(array):
        return lax.dynamic_slice_in_dim(array, feature_start, width_part, array.ndim - 1)

    row_mean = row_sum[:stat_rows].reshape(local_tokens, 1) / resid_in.shape[1]
    d_inputs = own_columns(d_mixed) + factor * (
        d_normed * own_columns(norm_attn) - own_columns(unit_rows) * row_mean
    )
    d_inputs = d_inputs.astype(jnp.bfloat16).reshape(1, local_tokens, width_part)
    small = small.reshape(-1)
    place = shard_index * n_ctx + lax.axis_index("ctx")
    full_width = 2 * width_half
    ranks = 2 * n_ctx

    def own_part(start, size):
        return lax.dynamic_slice_in_dim(
            small[start : start + size], place * (size // ranks), size // ranks, 0
        )

    gradients = (
        d_query,
        d_key,
        d_value,
        d_out.T,
        d_gate,
        d_up,
        d_down.T,
        own_part(0, full_width),
        own_part(full_width, full_width),
        own_part(2 * full_width, HEAD_SIZE),
        own_part(2 * full_width + HEAD_SIZE, HEAD_SIZE),
    )
    return (outputs, d_inputs) + tuple(gradients)


def solution(mesh):
    return jax.shard_map(
        partial(body, dict(mesh.shape)),
        mesh=mesh,
        in_specs=(
            P("shard", "ctx", "tp"),
            P("shard", "tp"),
            P("shard", "tp"),
            P("shard", "tp"),
            P("tp", "shard"),
            P("shard", "tp"),
            P("shard", "tp"),
            P("tp", "shard"),
            P("shard"),
            P("shard"),
            P("shard"),
            P("shard"),
            P("shard", "ctx", "tp"),
        ),
        out_specs=(
            P("shard", "ctx", "tp"),
            P("shard", "ctx", "tp"),
            P(("shard", "ctx"), "tp"),
            P(("shard", "ctx"), "tp"),
            P(("shard", "ctx"), "tp"),
            P("tp", ("shard", "ctx")),
            P(("shard", "ctx"), "tp"),
            P(("shard", "ctx"), "tp"),
            P("tp", ("shard", "ctx")),
            P(("shard", "ctx")),
            P(("shard", "ctx")),
            P(("shard", "ctx")),
            P(("shard", "ctx")),
        ),
        check_vma=False,
    )
```

```python
from functools import partial

import jax
import jax.numpy as jnp
from jax import lax
from jax.experimental import pallas as pl
from jax.experimental.pallas import tpu as pltpu
from jax.sharding import PartitionSpec as P

HEAD_SIZE = 128


epsilon = 1e-06
rope_base = 1000000.0
masked_score = -1e30


def rms_norm(value_rows, gain_row):
    return (
        value_rows
        * lax.rsqrt(jnp.mean(value_rows * value_rows, axis=-1, keepdims=True) + epsilon)
        * gain_row
    )


def rms_back(value_rows, gain_row, grad_in):
    factor = lax.rsqrt(jnp.mean(value_rows * value_rows, axis=-1, keepdims=True) + epsilon)
    unit_rows = value_rows * factor
    weighted = grad_in * gain_row
    d_values = factor * (
        weighted - unit_rows * jnp.mean(weighted * unit_rows, axis=-1, keepdims=True)
    )
    return (d_values, jnp.sum(grad_in * unit_rows, axis=0))


def rotary(value_rows, positions):
    half_dim = value_rows.shape[-1] // 2
    frequency = jnp.power(
        rope_base, -(jnp.arange(half_dim).astype(jnp.float32) * 2.0 / value_rows.shape[-1])
    )
    angles = positions[:, None] * frequency[None, :]
    cosine = jnp.concatenate([jnp.cos(angles), jnp.cos(angles)], axis=-1)[:, None, :]
    sine_part = jnp.concatenate([jnp.sin(angles), jnp.sin(angles)], axis=-1)[:, None, :]
    turned = jnp.concatenate([-value_rows[..., half_dim:], value_rows[..., :half_dim]], axis=-1)
    return value_rows * cosine + turned * sine_part


def head_prep(projected, gain_row, positions):
    tokens = projected.shape[0]
    shaped = projected.reshape(tokens, -1, HEAD_SIZE)
    return rotary(rms_norm(shaped, gain_row), positions).reshape(tokens, -1)


def query_block(array, head_index, heads_per_group):
    tokens = array.shape[0]
    piece = array[
        :, head_index * heads_per_group * HEAD_SIZE : (head_index + 1) * heads_per_group * HEAD_SIZE
    ]
    return (
        piece.reshape(tokens, heads_per_group, HEAD_SIZE)
        .transpose(1, 0, 2)
        .reshape(heads_per_group * tokens, HEAD_SIZE)
    )


def block_back(rows_in, heads_per_group):
    tokens = rows_in.shape[0] // heads_per_group
    return (
        rows_in.reshape(heads_per_group, tokens, HEAD_SIZE)
        .transpose(1, 0, 2)
        .reshape(tokens, heads_per_group * HEAD_SIZE)
    )


MESH_IDS = pl.DeviceIdType.MESH


def exchange(name, collective_id, sizes, ops):
    axes = []
    out_shapes = []
    scratch = []
    slots_of = []
    total = 0
    n_sems = 0
    for array, op_axes, kind, dim in ops:
        axes += op_axes
        shape = list(array.shape)
        slots_of.append(len(scratch))
        total += array.size
        n = sizes[op_axes[0]]
        dtype = array.dtype
        if kind == "gather":
            shape[dim] *= n
            n_sems += n
        elif kind == "pair":
            shape[dim] *= 2
            n_sems += 1
        elif kind == "scatter":
            shape[dim] //= n
            scratch.append(pltpu.VMEM((n, *shape), dtype))
            dtype = jnp.float32
            n_sems += n
        elif kind == "reduce":
            scratch.append(pltpu.VMEM((n, shape[0], shape[1] // n), dtype))
            n_sems += 2 * n
        elif kind == "grad":
            half = shape[0] // 2
            scratch.append(pltpu.VMEM((half, shape[1]), dtype))
            scratch.append(pltpu.VMEM((half, shape[1]), dtype))
            shape[0] = half // sizes["ctx"]
            scratch.append(pltpu.VMEM((sizes["ctx"], *shape), dtype))
            dtype = jnp.float32
            n_sems += 1 + sizes["ctx"]
        else:
            n_max = max(sizes[axis] for axis in op_axes)
            scratch.append(pltpu.VMEM((len(op_axes), *shape), dtype))
            scratch.append(pltpu.VMEM((len(op_axes), n_max, *shape), dtype))
            n_sems += sum(sizes[axis] for axis in op_axes)
        out_shapes.append(jax.ShapeDtypeStruct(tuple(shape), dtype))
    axes = tuple(dict.fromkeys(axes))
    count = len(ops)

    def kernel(*refs):
        ins = refs[:count]
        outs = refs[count : 2 * count]
        bufs = refs[2 * count : -2]
        send_sem, recv_sem = refs[-2:]
        barrier = pltpu.get_barrier_semaphore()
        n_peers = 0
        for axis in axes:
            n = sizes[axis]
            me = lax.axis_index(axis)
            for k in range(1, n):
                pl.semaphore_signal(
                    barrier, inc=1, device_id={axis: lax.rem(me + k, n)}, device_id_type=MESH_IDS
                )
                n_peers += 1
        pl.semaphore_wait(barrier, n_peers)
        sends = []
        used = [0]

        def send(src, dst, land, axis, peer):
            index = used[0]
            used[0] += 1
            make = partial(
                pltpu.make_async_remote_copy,
                src_ref=src,
                send_sem=send_sem.at[index],
                recv_sem=recv_sem.at[index],
                device_id={axis: peer},
                device_id_type=MESH_IDS,
            )
            copy = make(dst_ref=dst)
            copy.start()
            sends.append(copy)
            return make(dst_ref=land)

        def peers(axis):
            n = sizes[axis]
            me = lax.axis_index(axis)
            return [(k, lax.rem(me + k, n), lax.rem(me - k + n, n)) for k in range(1, n)]

        def place(ref, index, axis, dim, width):
            n = sizes[axis]
            if axis == "tp":
                index = lax.rem(index + lax.axis_index("shard") * (n // 2), n)
            start = pl.multiple_of(index * width, width)
            if dim == 0:
                return ref.at[pl.ds(start, width), :]
            return ref.at[:, pl.ds(start, width)]

        def total_send(i, stage, value):
            axis = ops[i][1][stage]
            sent, slots = bufs[slots_of[i] : slots_of[i] + 2]
            me = lax.axis_index(axis)
            sent[stage] = value
            slots[stage, me] = value
            return [
                send(sent.at[stage], slots.at[stage, me], slots.at[stage, source], axis, peer)
                for k, peer, source in peers(axis)
            ]

        def total_take(i, stage, pending):
            slots = bufs[slots_of[i] + 1]
            for copy in pending:
                copy.wait_recv()
            value = slots[stage, 0]
            for k in range(1, sizes[ops[i][1][stage]]):
                value = value + slots[stage, k]
            return value

        pending = {}
        kinds = {
            kind: [i for i in range(count) if ops[i][2] == kind]
            for kind in ("total", "reduce", "scatter", "gather", "pair", "grad")
        }
        for i in kinds["total"]:
            pending[i] = total_send(i, 0, ins[i][...])
        for i in kinds["reduce"] + kinds["scatter"]:
            array, (axis,), kind, dim = ops[i]
            width = array.shape[dim] // sizes[axis]
            buf = bufs[slots_of[i]]
            pending[i] = [
                send(place(ins[i], peer, axis, dim, width), buf.at[k], buf.at[k], axis, peer)
                for k, peer, source in peers(axis)
            ]
        for i in kinds["gather"]:
            array, (axis,), kind, dim = ops[i]
            width = array.shape[dim]
            me = lax.axis_index(axis)
            pending[i] = [
                send(
                    ins[i],
                    place(outs[i], me, axis, dim, width),
                    place(outs[i], source, axis, dim, width),
                    axis,
                    peer,
                )
                for k, peer, source in peers(axis)
            ]
        for i in kinds["pair"]:
            array, axis, kind, dim = ops[i]
            width = array.shape[dim]
            second_half = pl.ds(width, width)
            dst = outs[i].at[second_half, :] if dim == 0 else outs[i].at[:, second_half]
            pending[i] = [send(ins[i], dst, dst, "shard", 1 - lax.axis_index("shard"))]
        for i in kinds["grad"]:
            half = ops[i][0].shape[0] // 2
            came = bufs[slots_of[i]]
            other = 1 - lax.axis_index("shard")
            pending[i] = [send(ins[i].at[pl.ds(half, half), :], came, came, "shard", other)]
        for i in kinds["gather"]:
            array, (axis,), kind, dim = ops[i]
            me = lax.axis_index(axis)
            place(outs[i], me, axis, dim, array.shape[dim])[...] = ins[i][...]
        for i in kinds["pair"]:
            array, axis, kind, dim = ops[i]
            first_half = pl.ds(0, array.shape[dim])
            if dim == 0:
                outs[i][first_half, :] = ins[i][...]
            else:
                outs[i][:, first_half] = ins[i][...]
        for i in kinds["grad"]:
            half = ops[i][0].shape[0] // 2
            came, both, slots = bufs[slots_of[i] : slots_of[i] + 3]
            pending[i][0].wait_recv()
            both[...] = (
                ins[i][pl.ds(0, half), :].astype(jnp.float32) + came[...].astype(jnp.float32)
            ).astype(both.dtype)
            width = half // sizes["ctx"]
            pending[i] = [
                send(place(both, peer, "ctx", 0, width), slots.at[k], slots.at[k], "ctx", peer)
                for k, peer, source in peers("ctx")
            ]
        value = {}
        for i in kinds["total"]:
            value[i] = total_take(i, 0, pending[i])
            if len(ops[i][1]) > 1:
                pending[i] = total_send(i, 1, value[i])
        second = []
        for i in kinds["reduce"] + kinds["scatter"]:
            array, (axis,), kind, dim = ops[i]
            buf = bufs[slots_of[i]]
            me = lax.axis_index(axis)
            width = array.shape[dim] // sizes[axis]
            for copy in pending[i]:
                copy.wait_recv()
            summed = place(ins[i], me, axis, dim, width)[...].astype(jnp.float32)
            for k in range(1, sizes[axis]):
                summed = summed + buf[k].astype(jnp.float32)
            if kind == "scatter":
                outs[i][...] = summed
                continue
            mine = place(outs[i], me, axis, dim, width)
            mine[...] = summed.astype(array.dtype)
            second += [
                send(mine, mine, place(outs[i], source, axis, dim, width), axis, peer)
                for k, peer, source in peers(axis)
            ]
        for i in kinds["total"]:
            for stage in range(1, len(ops[i][1])):
                value[i] = total_take(i, stage, pending[i])
                if stage + 1 < len(ops[i][1]):
                    pending[i] = total_send(i, stage + 1, value[i])
            outs[i][...] = value[i]
        for i in kinds["grad"]:
            both, slots = bufs[slots_of[i] + 1 : slots_of[i] + 3]
            for copy in pending[i]:
                copy.wait_recv()
            width = slots.shape[1]
            summed = place(both, lax.axis_index("ctx"), "ctx", 0, width)[...].astype(jnp.float32)
            for k in range(1, sizes["ctx"]):
                summed = summed + slots[k].astype(jnp.float32)
            outs[i][...] = summed
        for i in kinds["gather"] + kinds["pair"]:
            second += pending[i]
        for copy in second:
            copy.wait_recv()
        for copy in sends:
            copy.wait_send()

    return pl.pallas_call(
        kernel,
        name=name,
        out_shape=tuple(out_shapes),
        in_specs=[pl.BlockSpec(memory_space=pltpu.VMEM)] * count,
        out_specs=tuple([pl.BlockSpec(memory_space=pltpu.VMEM)] * count),
        scratch_shapes=scratch
        + [pltpu.SemaphoreType.DMA((n_sems,)), pltpu.SemaphoreType.DMA((n_sems,))],
        compiler_params=pltpu.CompilerParams(
            collective_id=collective_id, has_side_effects=True, vmem_limit_bytes=32 * 1024 * 1024
        ),
        cost_estimate=pl.CostEstimate(flops=0, bytes_accessed=8 * total, transcendentals=0),
    )(*[op[0] for op in ops])


SHARD = ("shard",)
GRAD_AXES = ("shard", "ctx")
ALL_AXES = ("tp", "ctx", "shard")
TP = ("tp",)
CTX = ("ctx",)


def body(
    sizes,
    inputs,
    w_query,
    key_weight,
    value_weight,
    w_out,
    w_gate,
    w_up,
    w_down,
    norm_attn,
    norm_mlp,
    gain_query,
    gain_key,
    cotangent,
):
    n_ctx = sizes["ctx"]
    n_tp = sizes["tp"]
    shard_index = lax.axis_index("shard")
    width_half = norm_attn.shape[0]
    packed = jnp.concatenate([norm_attn, norm_mlp, gain_query, gain_key]).reshape(-1, HEAD_SIZE)
    pack_rows = packed.shape[0]
    packed = jnp.pad(packed, ((0, -pack_rows % 16), (0, 0)))
    local_tokens = inputs.shape[1]
    width_part = inputs.shape[2]
    offset = lax.axis_index("ctx") * local_tokens
    query_pos = offset + jnp.arange(local_tokens, dtype=jnp.int32)
    positions = query_pos.astype(jnp.float32)
    full_in, gains, w_query, key_weight, value_weight = exchange(
        "gather_inputs",
        0,
        sizes,
        [
            (inputs.reshape(local_tokens, width_part), TP, "gather", 1),
            (packed, SHARD, "gather", 0),
            (w_query, SHARD, "pair", 0),
            (key_weight, SHARD, "pair", 0),
            (value_weight, SHARD, "pair", 0),
        ],
    )
    gains = gains.reshape(2, -1).astype(jnp.float32)
    own_gains = jnp.where(shard_index == 0, gains[0], gains[1])
    other_gains = jnp.where(shard_index == 0, gains[1], gains[0])
    norm_attn = jnp.concatenate([own_gains[:width_half], other_gains[:width_half]])
    norm_mlp = jnp.concatenate(
        [own_gains[width_half : 2 * width_half], other_gains[width_half : 2 * width_half]]
    )
    small = 2 * width_half
    part = HEAD_SIZE // 2
    gain_query = gains[:, small : small + part].reshape(-1)
    gain_key = gains[:, small + part : small + 2 * part].reshape(-1)
    feature_start = lax.rem(lax.axis_index("tp") + shard_index * (n_tp // 2), n_tp) * width_part
    resid_in = full_in.astype(jnp.float32)
    normed_low = rms_norm(resid_in, norm_attn).astype(jnp.bfloat16)
    query_proj = jnp.dot(normed_low, w_query, preferred_element_type=jnp.float32)
    key_proj = jnp.dot(normed_low, key_weight, preferred_element_type=jnp.float32)
    value_proj = jnp.dot(normed_low, value_weight, preferred_element_type=jnp.float32)
    query_pull_fn = partial(head_prep, positions=positions)
    query_heads, query_pull = jax.vjp(query_pull_fn, query_proj, gain_query)
    key_heads, key_pull = jax.vjp(query_pull_fn, key_proj, gain_key)
    query_low = query_heads.astype(jnp.bfloat16)
    key_low = key_heads.astype(jnp.bfloat16)
    value_low = value_proj.astype(jnp.bfloat16)
    key_all, value_all, grad_out, w_out, w_gate, w_up, w_down = exchange(
        "gather_keys_values",
        1,
        sizes,
        [
            (key_low, CTX, "gather", 0),
            (value_low, CTX, "gather", 0),
            (cotangent.reshape(local_tokens, width_part), TP, "gather", 1),
            (w_out, SHARD, "pair", 1),
            (w_gate, SHARD, "pair", 0),
            (w_up, SHARD, "pair", 0),
            (w_down, SHARD, "pair", 1),
        ],
    )
    kv_local = key_low.shape[1] // HEAD_SIZE
    heads_per_group = query_low.shape[1] // (HEAD_SIZE * kv_local)
    seq_len = key_all.shape[0]
    key_pos = jnp.arange(seq_len, dtype=jnp.int32)
    causal = jnp.tile(query_pos[:, None] >= key_pos[None, :], (heads_per_group, 1))
    score_scale = HEAD_SIZE ** (-0.5)

    def head_scores(head_index):
        head_rows = query_block(query_low, head_index, heads_per_group)
        head_keys = key_all[:, head_index * HEAD_SIZE : (head_index + 1) * HEAD_SIZE]
        scores = (
            jnp.einsum("qd,kd->qk", head_rows, head_keys, preferred_element_type=jnp.float32)
            * score_scale
        )
        return (head_rows, head_keys, jnp.where(causal, scores, masked_score))

    attended_parts = []
    row_maxima = []
    row_totals = []
    for head_index in range(kv_local):
        head_rows, head_keys, scores = head_scores(head_index)
        row_max = jnp.max(scores, axis=1, keepdims=True)
        exp_scores = jnp.exp(scores - row_max)
        row_total = jnp.sum(exp_scores, axis=1, keepdims=True)
        probs_low = (exp_scores / row_total).astype(jnp.bfloat16)
        head_values = value_all[:, head_index * HEAD_SIZE : (head_index + 1) * HEAD_SIZE]
        head_out = jnp.dot(probs_low, head_values, preferred_element_type=jnp.float32)
        attended_parts.append(block_back(head_out, heads_per_group))
        row_maxima.append(row_max)
        row_totals.append(row_total)
    attended_low = jnp.concatenate(attended_parts, axis=1).astype(jnp.bfloat16)
    attn_part = jnp.dot(attended_low, w_out, preferred_element_type=jnp.float32)
    mixed = resid_in + exchange(
        "sum_attention", 2, sizes, [(attn_part.astype(jnp.bfloat16), TP, "reduce", 1)]
    )[0].astype(jnp.float32)
    normed_mlp_low = rms_norm(mixed, norm_mlp).astype(jnp.bfloat16)
    gate_act = jnp.dot(normed_mlp_low, w_gate, preferred_element_type=jnp.float32)
    up_act = jnp.dot(normed_mlp_low, w_up, preferred_element_type=jnp.float32)
    hidden_low = (jax.nn.silu(gate_act) * up_act).astype(jnp.bfloat16)
    mlp_part = jnp.dot(hidden_low, w_down, preferred_element_type=jnp.float32)
    d_down = jnp.einsum("tf,td->df", hidden_low, grad_out, preferred_element_type=jnp.float32)
    d_hidden = jnp.einsum("td,fd->tf", grad_out, w_down, preferred_element_type=jnp.float32)
    sigmoid_gate = jax.nn.sigmoid(gate_act)
    d_gate_low = (
        d_hidden * up_act * sigmoid_gate * (1.0 + gate_act * (1.0 - sigmoid_gate))
    ).astype(jnp.bfloat16)
    d_up_low = (d_hidden * gate_act * sigmoid_gate).astype(jnp.bfloat16)
    d_gate = jnp.einsum("td,tf->df", normed_mlp_low, d_gate_low, preferred_element_type=jnp.float32)
    d_up = jnp.einsum("td,tf->df", normed_mlp_low, d_up_low, preferred_element_type=jnp.float32)
    d_normed_mlp = jnp.einsum("tf,df->td", d_gate_low, w_gate, preferred_element_type=jnp.float32)
    d_normed_mlp = d_normed_mlp + jnp.einsum(
        "tf,df->td", d_up_low, w_up, preferred_element_type=jnp.float32
    )
    d_normed_mlp, d_down, d_gate, d_up = exchange(
        "sum_feed_forward",
        3,
        sizes,
        [
            (d_normed_mlp.astype(jnp.bfloat16), TP, "reduce", 1),
            (d_down.astype(jnp.bfloat16), GRAD_AXES, "grad", 0),
            (d_gate.astype(jnp.bfloat16), GRAD_AXES, "grad", 0),
            (d_up.astype(jnp.bfloat16), GRAD_AXES, "grad", 0),
        ],
    )
    d_normed_mlp = d_normed_mlp.astype(jnp.float32)
    d_mix_norm, d_norm_mlp = rms_back(mixed, norm_mlp, d_normed_mlp)
    d_mixed = grad_out.astype(jnp.float32) + d_mix_norm
    d_mixed_low = d_mixed.astype(jnp.bfloat16)
    d_out = jnp.einsum("th,td->dh", attended_low, d_mixed_low, preferred_element_type=jnp.float32)
    d_attended = jnp.einsum(
        "td,hd->th", d_mixed_low, w_out, preferred_element_type=jnp.float32
    ).astype(jnp.bfloat16)
    d_query_parts = []
    d_key_parts = []
    d_value_parts = []
    for head_index in range(kv_local):
        head_rows, head_keys, scores = head_scores(head_index)
        probs_full = jnp.exp(scores - row_maxima[head_index]) / row_totals[head_index]
        probs_low = probs_full.astype(jnp.bfloat16)
        head_values = value_all[:, head_index * HEAD_SIZE : (head_index + 1) * HEAD_SIZE]
        d_rows = query_block(d_attended, head_index, heads_per_group)
        d_probs = jnp.einsum("qd,kd->qk", d_rows, head_values, preferred_element_type=jnp.float32)
        d_value_parts.append(
            jnp.einsum("qk,qd->kd", probs_low, d_rows, preferred_element_type=jnp.float32)
        )
        inner_sum = jnp.sum(probs_full * d_probs, axis=1, keepdims=True)
        d_scores = (probs_full * (d_probs - inner_sum)).astype(jnp.bfloat16)
        d_head_rows = jnp.dot(d_scores, head_keys, preferred_element_type=jnp.float32) * score_scale
        d_query_parts.append(block_back(d_head_rows, heads_per_group))
        d_key_parts.append(
            jnp.einsum("qk,qd->kd", d_scores, head_rows, preferred_element_type=jnp.float32)
            * score_scale
        )
    d_query_heads = jnp.concatenate(d_query_parts, axis=1)
    d_keys_all = jnp.concatenate(d_key_parts, axis=1)
    d_values_all = jnp.concatenate(d_value_parts, axis=1)
    d_key_heads, d_value_proj, mlp_sum = exchange(
        "sum_keys_values",
        4,
        sizes,
        [
            (d_keys_all.astype(jnp.bfloat16), CTX, "scatter", 0),
            (d_values_all.astype(jnp.bfloat16), CTX, "scatter", 0),
            (mlp_part.astype(jnp.bfloat16), TP, "scatter", 1),
        ],
    )
    outputs = (
        (lax.dynamic_slice_in_dim(mixed, feature_start, width_part, 1) + mlp_sum)
        .astype(jnp.bfloat16)
        .reshape(1, local_tokens, width_part)
    )
    d_query_proj, d_gain_query = query_pull(d_query_heads)
    d_key_proj, d_gain_key = key_pull(d_key_heads)
    d_query_low = d_query_proj.astype(jnp.bfloat16)
    d_key_low = d_key_proj.astype(jnp.bfloat16)
    d_value_low = d_value_proj.astype(jnp.bfloat16)
    d_query = jnp.einsum("td,th->dh", normed_low, d_query_low, preferred_element_type=jnp.float32)
    d_key = jnp.einsum("td,th->dh", normed_low, d_key_low, preferred_element_type=jnp.float32)
    d_value = jnp.einsum("td,th->dh", normed_low, d_value_low, preferred_element_type=jnp.float32)
    d_normed = jnp.einsum("th,dh->td", d_query_low, w_query, preferred_element_type=jnp.float32)
    d_normed = d_normed + jnp.einsum(
        "th,dh->td", d_key_low, key_weight, preferred_element_type=jnp.float32
    )
    d_normed = d_normed + jnp.einsum(
        "th,dh->td", d_value_low, value_weight, preferred_element_type=jnp.float32
    )
    factor = lax.rsqrt(jnp.mean(resid_in * resid_in, axis=-1, keepdims=True) + epsilon)
    unit_rows = resid_in * factor
    weighed = d_normed * unit_rows
    d_norm_attn = jnp.sum(weighed, axis=0)
    row_part = jnp.sum(weighed * norm_attn, axis=-1).reshape(-1, 128)
    stat_rows = row_part.shape[0]
    row_part = jnp.pad(row_part, ((0, -stat_rows % 8), (0, 0)))
    norms = jnp.stack([d_norm_attn, d_norm_mlp * (1.0 / n_tp)]).reshape(2, 2, width_half)
    norms = jnp.where(shard_index == 0, norms, norms[:, ::-1]).reshape(-1)
    small = jnp.concatenate([norms, d_gain_query, d_gain_key]).reshape(-1, HEAD_SIZE)
    small = jnp.pad(small, ((0, -small.shape[0] % 8), (0, 0)))
    row_sum, small, d_normed, d_out, d_query, d_key, d_value = exchange(
        "sum_input_gradient",
        5,
        sizes,
        [
            (row_part, TP, "total", 0),
            (small, ALL_AXES, "total", 0),
            (d_normed.astype(jnp.bfloat16), TP, "scatter", 1),
            (d_out.astype(jnp.bfloat16), GRAD_AXES, "grad", 0),
            (d_query.astype(jnp.bfloat16), GRAD_AXES, "grad", 0),
            (d_key.astype(jnp.bfloat16), GRAD_AXES, "grad", 0),
            (d_value.astype(jnp.bfloat16), GRAD_AXES, "grad", 0),
        ],
    )

    def own_columns(array):
        return lax.dynamic_slice_in_dim(array, feature_start, width_part, array.ndim - 1)

    row_mean = row_sum[:stat_rows].reshape(local_tokens, 1) / resid_in.shape[1]
    d_inputs = own_columns(d_mixed) + factor * (
        d_normed * own_columns(norm_attn) - own_columns(unit_rows) * row_mean
    )
    d_inputs = d_inputs.astype(jnp.bfloat16).reshape(1, local_tokens, width_part)
    small = small.reshape(-1)
    place = shard_index * n_ctx + lax.axis_index("ctx")
    full_width = 2 * width_half
    ranks = 2 * n_ctx

    def own_part(start, size):
        return lax.dynamic_slice_in_dim(
            small[start : start + size], place * (size // ranks), size // ranks, 0
        )

    gradients = (
        d_query,
        d_key,
        d_value,
        d_out.T,
        d_gate,
        d_up,
        d_down.T,
        own_part(0, full_width),
        own_part(full_width, full_width),
        own_part(2 * full_width, HEAD_SIZE),
        own_part(2 * full_width + HEAD_SIZE, HEAD_SIZE),
    )
    return (outputs, d_inputs) + tuple(gradients)


def solution(mesh):
    return jax.shard_map(
        partial(body, dict(mesh.shape)),
        mesh=mesh,
        in_specs=(
            P("shard", "ctx", "tp"),
            P("shard", "tp"),
            P("shard", "tp"),
            P("shard", "tp"),
            P("tp", "shard"),
            P("shard", "tp"),
            P("shard", "tp"),
            P("tp", "shard"),
            P("shard"),
            P("shard"),
            P("shard"),
            P("shard"),
            P("shard", "ctx", "tp"),
        ),
        out_specs=(
            P("shard", "ctx", "tp"),
            P("shard", "ctx", "tp"),
            P(("shard", "ctx"), "tp"),
            P(("shard", "ctx"), "tp"),
            P(("shard", "ctx"), "tp"),
            P("tp", ("shard", "ctx")),
            P(("shard", "ctx"), "tp"),
            P(("shard", "ctx"), "tp"),
            P("tp", ("shard", "ctx")),
            P(("shard", "ctx")),
            P(("shard", "ctx")),
            P(("shard", "ctx")),
            P(("shard", "ctx")),
        ),
        check_vma=False,
    )
```

```python
from functools import partial

import jax
import jax.numpy as jnp
from jax import lax
from jax.experimental import pallas as pl
from jax.experimental.pallas import tpu as pltpu
from jax.sharding import PartitionSpec as P

HEAD_SIZE = 128


epsilon = 1e-06
rope_base = 1000000.0
masked_score = -1e30


def rms_norm(value_rows, gain_row):
    return (
        value_rows
        * lax.rsqrt(jnp.mean(value_rows * value_rows, axis=-1, keepdims=True) + epsilon)
        * gain_row
    )


def rms_back(value_rows, gain_row, grad_in):
    factor = lax.rsqrt(jnp.mean(value_rows * value_rows, axis=-1, keepdims=True) + epsilon)
    unit_rows = value_rows * factor
    weighted = grad_in * gain_row
    d_values = factor * (
        weighted - unit_rows * jnp.mean(weighted * unit_rows, axis=-1, keepdims=True)
    )
    return (d_values, jnp.sum(grad_in * unit_rows, axis=0))


def rotary(value_rows, positions):
    half_dim = value_rows.shape[-1] // 2
    frequency = jnp.power(
        rope_base, -(jnp.arange(half_dim).astype(jnp.float32) * 2.0 / value_rows.shape[-1])
    )
    angles = positions[:, None] * frequency[None, :]
    cosine = jnp.concatenate([jnp.cos(angles), jnp.cos(angles)], axis=-1)[:, None, :]
    sine_part = jnp.concatenate([jnp.sin(angles), jnp.sin(angles)], axis=-1)[:, None, :]
    turned = jnp.concatenate([-value_rows[..., half_dim:], value_rows[..., :half_dim]], axis=-1)
    return value_rows * cosine + turned * sine_part


def head_prep(projected, gain_row, positions):
    tokens = projected.shape[0]
    shaped = projected.reshape(tokens, -1, HEAD_SIZE)
    return rotary(rms_norm(shaped, gain_row), positions).reshape(tokens, -1)


def query_block(array, head_index, heads_per_group):
    tokens = array.shape[0]
    piece = array[
        :, head_index * heads_per_group * HEAD_SIZE : (head_index + 1) * heads_per_group * HEAD_SIZE
    ]
    return (
        piece.reshape(tokens, heads_per_group, HEAD_SIZE)
        .transpose(1, 0, 2)
        .reshape(heads_per_group * tokens, HEAD_SIZE)
    )


def block_back(rows_in, heads_per_group):
    tokens = rows_in.shape[0] // heads_per_group
    return (
        rows_in.reshape(heads_per_group, tokens, HEAD_SIZE)
        .transpose(1, 0, 2)
        .reshape(tokens, heads_per_group * HEAD_SIZE)
    )


MESH_IDS = pl.DeviceIdType.MESH


def exchange(name, collective_id, sizes, ops):
    axes = []
    out_shapes = []
    scratch = []
    slots_of = []
    total = 0
    n_sems = 0
    for array, op_axes, kind, dim in ops:
        axes += op_axes
        shape = list(array.shape)
        slots_of.append(len(scratch))
        total += array.size
        n = sizes[op_axes[0]]
        dtype = array.dtype
        if kind == "gather":
            shape[dim] *= n
            n_sems += n
        elif kind == "pair":
            shape[dim] *= 2
            n_sems += 1
        elif kind == "scatter":
            shape[dim] //= n
            scratch.append(pltpu.VMEM((n, *shape), dtype))
            dtype = jnp.float32
            n_sems += n
        elif kind == "reduce":
            scratch.append(pltpu.VMEM((n, shape[0], shape[1] // n), dtype))
            n_sems += 2 * n
        elif kind == "grad":
            half = shape[0] // 2
            scratch.append(pltpu.VMEM((half, shape[1]), dtype))
            scratch.append(pltpu.VMEM((half, shape[1]), dtype))
            shape[0] = half // sizes["ctx"]
            scratch.append(pltpu.VMEM((sizes["ctx"], *shape), dtype))
            dtype = jnp.float32
            n_sems += 1 + sizes["ctx"]
        else:
            n_max = max(sizes[axis] for axis in op_axes)
            scratch.append(pltpu.VMEM((len(op_axes), *shape), dtype))
            scratch.append(pltpu.VMEM((len(op_axes), n_max, *shape), dtype))
            n_sems += sum(sizes[axis] for axis in op_axes)
        out_shapes.append(jax.ShapeDtypeStruct(tuple(shape), dtype))
    axes = tuple(dict.fromkeys(axes))
    count = len(ops)

    def kernel(*refs):
        ins = refs[:count]
        outs = refs[count : 2 * count]
        bufs = refs[2 * count : -2]
        send_sem, recv_sem = refs[-2:]
        barrier = pltpu.get_barrier_semaphore()
        n_peers = 0
        for axis in axes:
            n = sizes[axis]
            me = lax.axis_index(axis)
            for k in range(1, n):
                pl.semaphore_signal(
                    barrier, inc=1, device_id={axis: lax.rem(me + k, n)}, device_id_type=MESH_IDS
                )
                n_peers += 1
        pl.semaphore_wait(barrier, n_peers)
        sends = []
        used = [0]

        def send(src, dst, land, axis, peer):
            index = used[0]
            used[0] += 1
            make = partial(
                pltpu.make_async_remote_copy,
                src_ref=src,
                send_sem=send_sem.at[index],
                recv_sem=recv_sem.at[index],
                device_id={axis: peer},
                device_id_type=MESH_IDS,
            )
            copy = make(dst_ref=dst)
            copy.start()
            sends.append(copy)
            return make(dst_ref=land)

        def peers(axis):
            n = sizes[axis]
            me = lax.axis_index(axis)
            return [(k, lax.rem(me + k, n), lax.rem(me - k + n, n)) for k in range(1, n)]

        def place(ref, index, axis, dim, width):
            n = sizes[axis]
            if axis == "tp":
                index = lax.rem(index + lax.axis_index("shard") * (n // 2), n)
            start = pl.multiple_of(index * width, width)
            if dim == 0:
                return ref.at[pl.ds(start, width), :]
            return ref.at[:, pl.ds(start, width)]

        def total_send(i, stage, value):
            axis = ops[i][1][stage]
            sent, slots = bufs[slots_of[i] : slots_of[i] + 2]
            me = lax.axis_index(axis)
            sent[stage] = value
            slots[stage, me] = value
            return [
                send(sent.at[stage], slots.at[stage, me], slots.at[stage, source], axis, peer)
                for k, peer, source in peers(axis)
            ]

        def total_take(i, stage, pending):
            slots = bufs[slots_of[i] + 1]
            for copy in pending:
                copy.wait_recv()
            value = slots[stage, 0]
            for k in range(1, sizes[ops[i][1][stage]]):
                value = value + slots[stage, k]
            return value

        pending = {}
        kinds = {
            kind: [i for i in range(count) if ops[i][2] == kind]
            for kind in ("total", "reduce", "scatter", "gather", "pair", "grad")
        }
        for i in kinds["total"]:
            pending[i] = total_send(i, 0, ins[i][...])
        for i in kinds["reduce"] + kinds["scatter"]:
            array, (axis,), kind, dim = ops[i]
            width = array.shape[dim] // sizes[axis]
            buf = bufs[slots_of[i]]
            pending[i] = [
                send(place(ins[i], peer, axis, dim, width), buf.at[k], buf.at[k], axis, peer)
                for k, peer, source in peers(axis)
            ]
        for i in kinds["gather"]:
            array, (axis,), kind, dim = ops[i]
            width = array.shape[dim]
            me = lax.axis_index(axis)
            pending[i] = [
                send(
                    ins[i],
                    place(outs[i], me, axis, dim, width),
                    place(outs[i], source, axis, dim, width),
                    axis,
                    peer,
                )
                for k, peer, source in peers(axis)
            ]
        for i in kinds["pair"]:
            array, axis, kind, dim = ops[i]
            width = array.shape[dim]
            second_half = pl.ds(width, width)
            dst = outs[i].at[second_half, :] if dim == 0 else outs[i].at[:, second_half]
            pending[i] = [send(ins[i], dst, dst, "shard", 1 - lax.axis_index("shard"))]
        for i in kinds["grad"]:
            half = ops[i][0].shape[0] // 2
            came = bufs[slots_of[i]]
            other = 1 - lax.axis_index("shard")
            pending[i] = [send(ins[i].at[pl.ds(half, half), :], came, came, "shard", other)]
        for i in kinds["gather"]:
            array, (axis,), kind, dim = ops[i]
            me = lax.axis_index(axis)
            place(outs[i], me, axis, dim, array.shape[dim])[...] = ins[i][...]
        for i in kinds["pair"]:
            array, axis, kind, dim = ops[i]
            first_half = pl.ds(0, array.shape[dim])
            if dim == 0:
                outs[i][first_half, :] = ins[i][...]
            else:
                outs[i][:, first_half] = ins[i][...]
        for i in kinds["grad"]:
            half = ops[i][0].shape[0] // 2
            came, both, slots = bufs[slots_of[i] : slots_of[i] + 3]
            pending[i][0].wait_recv()
            both[...] = (
                ins[i][pl.ds(0, half), :].astype(jnp.float32) + came[...].astype(jnp.float32)
            ).astype(both.dtype)
            width = half // sizes["ctx"]
            pending[i] = [
                send(place(both, peer, "ctx", 0, width), slots.at[k], slots.at[k], "ctx", peer)
                for k, peer, source in peers("ctx")
            ]
        value = {}
        for i in kinds["total"]:
            value[i] = total_take(i, 0, pending[i])
            if len(ops[i][1]) > 1:
                pending[i] = total_send(i, 1, value[i])
        second = []
        for i in kinds["reduce"] + kinds["scatter"]:
            array, (axis,), kind, dim = ops[i]
            buf = bufs[slots_of[i]]
            me = lax.axis_index(axis)
            width = array.shape[dim] // sizes[axis]
            for copy in pending[i]:
                copy.wait_recv()
            summed = place(ins[i], me, axis, dim, width)[...].astype(jnp.float32)
            for k in range(1, sizes[axis]):
                summed = summed + buf[k].astype(jnp.float32)
            if kind == "scatter":
                outs[i][...] = summed
                continue
            mine = place(outs[i], me, axis, dim, width)
            mine[...] = summed.astype(array.dtype)
            second += [
                send(mine, mine, place(outs[i], source, axis, dim, width), axis, peer)
                for k, peer, source in peers(axis)
            ]
        for i in kinds["total"]:
            for stage in range(1, len(ops[i][1])):
                value[i] = total_take(i, stage, pending[i])
                if stage + 1 < len(ops[i][1]):
                    pending[i] = total_send(i, stage + 1, value[i])
            outs[i][...] = value[i]
        for i in kinds["grad"]:
            both, slots = bufs[slots_of[i] + 1 : slots_of[i] + 3]
            for copy in pending[i]:
                copy.wait_recv()
            width = slots.shape[1]
            summed = place(both, lax.axis_index("ctx"), "ctx", 0, width)[...].astype(jnp.float32)
            for k in range(1, sizes["ctx"]):
                summed = summed + slots[k].astype(jnp.float32)
            outs[i][...] = summed
        for i in kinds["gather"] + kinds["pair"]:
            second += pending[i]
        for copy in second:
            copy.wait_recv()
        for copy in sends:
            copy.wait_send()

    return pl.pallas_call(
        kernel,
        name=name,
        out_shape=tuple(out_shapes),
        in_specs=[pl.BlockSpec(memory_space=pltpu.VMEM)] * count,
        out_specs=tuple([pl.BlockSpec(memory_space=pltpu.VMEM)] * count),
        scratch_shapes=scratch
        + [pltpu.SemaphoreType.DMA((n_sems,)), pltpu.SemaphoreType.DMA((n_sems,))],
        compiler_params=pltpu.CompilerParams(
            collective_id=collective_id, has_side_effects=True, vmem_limit_bytes=32 * 1024 * 1024
        ),
        cost_estimate=pl.CostEstimate(flops=0, bytes_accessed=8 * total, transcendentals=0),
    )(*[op[0] for op in ops])


SHARD = ("shard",)
GRAD_AXES = ("shard", "ctx")
ALL_AXES = ("tp", "ctx", "shard")
TP = ("tp",)
CTX = ("ctx",)


def body(
    sizes,
    inputs,
    w_query,
    key_weight,
    value_weight,
    w_out,
    w_gate,
    w_up,
    w_down,
    norm_attn,
    norm_mlp,
    gain_query,
    gain_key,
    cotangent,
):
    n_ctx = sizes["ctx"]
    n_tp = sizes["tp"]
    shard_index = lax.axis_index("shard")
    width_half = norm_attn.shape[0]
    packed = jnp.concatenate([norm_attn, norm_mlp, gain_query, gain_key]).reshape(-1, HEAD_SIZE)
    pack_rows = packed.shape[0]
    packed = jnp.pad(packed, ((0, -pack_rows % 16), (0, 0)))
    local_tokens = inputs.shape[1]
    width_part = inputs.shape[2]
    offset = lax.axis_index("ctx") * local_tokens
    query_pos = offset + jnp.arange(local_tokens, dtype=jnp.int32)
    positions = query_pos.astype(jnp.float32)
    full_in, gains, w_query, key_weight, value_weight = exchange(
        "gather_inputs",
        0,
        sizes,
        [
            (inputs.reshape(local_tokens, width_part), TP, "gather", 1),
            (packed, SHARD, "gather", 0),
            (w_query, SHARD, "pair", 0),
            (key_weight, SHARD, "pair", 0),
            (value_weight, SHARD, "pair", 0),
        ],
    )
    gains = gains.reshape(2, -1).astype(jnp.float32)
    own_gains = jnp.where(shard_index == 0, gains[0], gains[1])
    other_gains = jnp.where(shard_index == 0, gains[1], gains[0])
    norm_attn = jnp.concatenate([own_gains[:width_half], other_gains[:width_half]])
    norm_mlp = jnp.concatenate(
        [own_gains[width_half : 2 * width_half], other_gains[width_half : 2 * width_half]]
    )
    small = 2 * width_half
    part = HEAD_SIZE // 2
    gain_query = gains[:, small : small + part].reshape(-1)
    gain_key = gains[:, small + part : small + 2 * part].reshape(-1)
    feature_start = lax.rem(lax.axis_index("tp") + shard_index * (n_tp // 2), n_tp) * width_part
    resid_in = full_in.astype(jnp.float32)
    normed_low = rms_norm(resid_in, norm_attn).astype(jnp.bfloat16)
    query_proj = jnp.dot(normed_low, w_query, preferred_element_type=jnp.float32)
    key_proj = jnp.dot(normed_low, key_weight, preferred_element_type=jnp.float32)
    value_proj = jnp.dot(normed_low, value_weight, preferred_element_type=jnp.float32)
    query_pull_fn = partial(head_prep, positions=positions)
    query_heads, query_pull = jax.vjp(query_pull_fn, query_proj, gain_query)
    key_heads, key_pull = jax.vjp(query_pull_fn, key_proj, gain_key)
    query_low = query_heads.astype(jnp.bfloat16)
    key_low = key_heads.astype(jnp.bfloat16)
    value_low = value_proj.astype(jnp.bfloat16)
    key_all, value_all, grad_out, w_out, w_gate, w_up, w_down = exchange(
        "gather_keys_values",
        1,
        sizes,
        [
            (key_low, CTX, "gather", 0),
            (value_low, CTX, "gather", 0),
            (cotangent.reshape(local_tokens, width_part), TP, "gather", 1),
            (w_out, SHARD, "pair", 1),
            (w_gate, SHARD, "pair", 0),
            (w_up, SHARD, "pair", 0),
            (w_down, SHARD, "pair", 1),
        ],
    )
    kv_local = key_low.shape[1] // HEAD_SIZE
    heads_per_group = query_low.shape[1] // (HEAD_SIZE * kv_local)
    seq_len = key_all.shape[0]
    key_pos = jnp.arange(seq_len, dtype=jnp.int32)
    causal = jnp.tile(query_pos[:, None] >= key_pos[None, :], (heads_per_group, 1))
    score_scale = HEAD_SIZE ** (-0.5)

    def head_scores(head_index):
        head_rows = query_block(query_low, head_index, heads_per_group)
        head_keys = key_all[:, head_index * HEAD_SIZE : (head_index + 1) * HEAD_SIZE]
        scores = (
            jnp.einsum("qd,kd->qk", head_rows, head_keys, preferred_element_type=jnp.float32)
            * score_scale
        )
        return (head_rows, head_keys, jnp.where(causal, scores, masked_score))

    attended_parts = []
    row_maxima = []
    row_totals = []
    for head_index in range(kv_local):
        head_rows, head_keys, scores = head_scores(head_index)
        row_max = jnp.max(scores, axis=1, keepdims=True)
        exp_scores = jnp.exp(scores - row_max)
        row_total = jnp.sum(exp_scores, axis=1, keepdims=True)
        probs_low = (exp_scores / row_total).astype(jnp.bfloat16)
        head_values = value_all[:, head_index * HEAD_SIZE : (head_index + 1) * HEAD_SIZE]
        head_out = jnp.dot(probs_low, head_values, preferred_element_type=jnp.float32)
        attended_parts.append(block_back(head_out, heads_per_group))
        row_maxima.append(row_max)
        row_totals.append(row_total)
    attended_low = jnp.concatenate(attended_parts, axis=1).astype(jnp.bfloat16)
    attn_part = jnp.dot(attended_low, w_out, preferred_element_type=jnp.float32)
    mixed = resid_in + exchange(
        "sum_attention", 2, sizes, [(attn_part.astype(jnp.bfloat16), TP, "reduce", 1)]
    )[0].astype(jnp.float32)
    normed_mlp_low = rms_norm(mixed, norm_mlp).astype(jnp.bfloat16)
    gate_act = jnp.dot(normed_mlp_low, w_gate, preferred_element_type=jnp.float32)
    up_act = jnp.dot(normed_mlp_low, w_up, preferred_element_type=jnp.float32)
    hidden_low = (jax.nn.silu(gate_act) * up_act).astype(jnp.bfloat16)
    mlp_part = jnp.dot(hidden_low, w_down, preferred_element_type=jnp.float32)
    d_down = jnp.einsum("tf,td->df", hidden_low, grad_out, preferred_element_type=jnp.float32)
    d_hidden = jnp.einsum("td,fd->tf", grad_out, w_down, preferred_element_type=jnp.float32)
    sigmoid_gate = jax.nn.sigmoid(gate_act)
    d_gate_low = (
        d_hidden * up_act * sigmoid_gate * (1.0 + gate_act * (1.0 - sigmoid_gate))
    ).astype(jnp.bfloat16)
    d_up_low = (d_hidden * gate_act * sigmoid_gate).astype(jnp.bfloat16)
    d_gate = jnp.einsum("td,tf->df", normed_mlp_low, d_gate_low, preferred_element_type=jnp.float32)
    d_up = jnp.einsum("td,tf->df", normed_mlp_low, d_up_low, preferred_element_type=jnp.float32)
    d_normed_mlp = jnp.einsum("tf,df->td", d_gate_low, w_gate, preferred_element_type=jnp.float32)
    d_normed_mlp = d_normed_mlp + jnp.einsum(
        "tf,df->td", d_up_low, w_up, preferred_element_type=jnp.float32
    )
    d_normed_mlp, d_down, d_gate, d_up = exchange(
        "sum_feed_forward",
        3,
        sizes,
        [
            (d_normed_mlp.astype(jnp.bfloat16), TP, "reduce", 1),
            (d_down.astype(jnp.bfloat16), GRAD_AXES, "grad", 0),
            (d_gate.astype(jnp.bfloat16), GRAD_AXES, "grad", 0),
            (d_up.astype(jnp.bfloat16), GRAD_AXES, "grad", 0),
        ],
    )
    d_normed_mlp = d_normed_mlp.astype(jnp.float32)
    d_mix_norm, d_norm_mlp = rms_back(mixed, norm_mlp, d_normed_mlp)
    d_mixed = grad_out.astype(jnp.float32) + d_mix_norm
    d_mixed_low = d_mixed.astype(jnp.bfloat16)
    d_out = jnp.einsum("th,td->dh", attended_low, d_mixed_low, preferred_element_type=jnp.float32)
    d_attended = jnp.einsum(
        "td,hd->th", d_mixed_low, w_out, preferred_element_type=jnp.float32
    ).astype(jnp.bfloat16)
    d_query_parts = []
    d_key_parts = []
    d_value_parts = []
    for head_index in range(kv_local):
        head_rows, head_keys, scores = head_scores(head_index)
        probs_full = jnp.exp(scores - row_maxima[head_index]) / row_totals[head_index]
        probs_low = probs_full.astype(jnp.bfloat16)
        head_values = value_all[:, head_index * HEAD_SIZE : (head_index + 1) * HEAD_SIZE]
        d_rows = query_block(d_attended, head_index, heads_per_group)
        d_probs = jnp.einsum("qd,kd->qk", d_rows, head_values, preferred_element_type=jnp.float32)
        d_value_parts.append(
            jnp.einsum("qk,qd->kd", probs_low, d_rows, preferred_element_type=jnp.float32)
        )
        inner_sum = jnp.sum(probs_full * d_probs, axis=1, keepdims=True)
        d_scores = (probs_full * (d_probs - inner_sum)).astype(jnp.bfloat16)
        d_head_rows = jnp.dot(d_scores, head_keys, preferred_element_type=jnp.float32) * score_scale
        d_query_parts.append(block_back(d_head_rows, heads_per_group))
        d_key_parts.append(
            jnp.einsum("qk,qd->kd", d_scores, head_rows, preferred_element_type=jnp.float32)
            * score_scale
        )
    d_query_heads = jnp.concatenate(d_query_parts, axis=1)
    d_keys_all = jnp.concatenate(d_key_parts, axis=1)
    d_values_all = jnp.concatenate(d_value_parts, axis=1)
    d_key_heads, d_value_proj = exchange(
        "sum_keys_values",
        4,
        sizes,
        [
            (d_keys_all.astype(jnp.bfloat16), CTX, "scatter", 0),
            (d_values_all.astype(jnp.bfloat16), CTX, "scatter", 0),
        ],
    )
    d_query_proj, d_gain_query = query_pull(d_query_heads)
    d_key_proj, d_gain_key = key_pull(d_key_heads)
    d_query_low = d_query_proj.astype(jnp.bfloat16)
    d_key_low = d_key_proj.astype(jnp.bfloat16)
    d_value_low = d_value_proj.astype(jnp.bfloat16)
    d_query = jnp.einsum("td,th->dh", normed_low, d_query_low, preferred_element_type=jnp.float32)
    d_key = jnp.einsum("td,th->dh", normed_low, d_key_low, preferred_element_type=jnp.float32)
    d_value = jnp.einsum("td,th->dh", normed_low, d_value_low, preferred_element_type=jnp.float32)
    d_normed = jnp.einsum("th,dh->td", d_query_low, w_query, preferred_element_type=jnp.float32)
    d_normed = d_normed + jnp.einsum(
        "th,dh->td", d_key_low, key_weight, preferred_element_type=jnp.float32
    )
    d_normed = d_normed + jnp.einsum(
        "th,dh->td", d_value_low, value_weight, preferred_element_type=jnp.float32
    )
    factor = lax.rsqrt(jnp.mean(resid_in * resid_in, axis=-1, keepdims=True) + epsilon)
    unit_rows = resid_in * factor
    weighed = d_normed * unit_rows
    d_norm_attn = jnp.sum(weighed, axis=0)
    row_part = jnp.sum(weighed * norm_attn, axis=-1).reshape(-1, 128)
    stat_rows = row_part.shape[0]
    row_part = jnp.pad(row_part, ((0, -stat_rows % 8), (0, 0)))
    norms = jnp.stack([d_norm_attn, d_norm_mlp * (1.0 / n_tp)]).reshape(2, 2, width_half)
    norms = jnp.where(shard_index == 0, norms, norms[:, ::-1]).reshape(-1)
    small = jnp.concatenate([norms, d_gain_query, d_gain_key]).reshape(-1, HEAD_SIZE)
    small = jnp.pad(small, ((0, -small.shape[0] % 8), (0, 0)))
    row_sum, small, d_normed, mlp_sum, d_out, d_query, d_key, d_value = exchange(
        "sum_input_gradient",
        5,
        sizes,
        [
            (row_part, TP, "total", 0),
            (small, ALL_AXES, "total", 0),
            (d_normed.astype(jnp.bfloat16), TP, "scatter", 1),
            (mlp_part.astype(jnp.bfloat16), TP, "scatter", 1),
            (d_out.astype(jnp.bfloat16), GRAD_AXES, "grad", 0),
            (d_query.astype(jnp.bfloat16), GRAD_AXES, "grad", 0),
            (d_key.astype(jnp.bfloat16), GRAD_AXES, "grad", 0),
            (d_value.astype(jnp.bfloat16), GRAD_AXES, "grad", 0),
        ],
    )

    outputs = (
        (lax.dynamic_slice_in_dim(mixed, feature_start, width_part, 1) + mlp_sum)
        .astype(jnp.bfloat16)
        .reshape(1, local_tokens, width_part)
    )

    def own_columns(array):
        return lax.dynamic_slice_in_dim(array, feature_start, width_part, array.ndim - 1)

    row_mean = row_sum[:stat_rows].reshape(local_tokens, 1) / resid_in.shape[1]
    d_inputs = own_columns(d_mixed) + factor * (
        d_normed * own_columns(norm_attn) - own_columns(unit_rows) * row_mean
    )
    d_inputs = d_inputs.astype(jnp.bfloat16).reshape(1, local_tokens, width_part)
    small = small.reshape(-1)
    place = shard_index * n_ctx + lax.axis_index("ctx")
    full_width = 2 * width_half
    ranks = 2 * n_ctx

    def own_part(start, size):
        return lax.dynamic_slice_in_dim(
            small[start : start + size], place * (size // ranks), size // ranks, 0
        )

    gradients = (
        d_query,
        d_key,
        d_value,
        d_out.T,
        d_gate,
        d_up,
        d_down.T,
        own_part(0, full_width),
        own_part(full_width, full_width),
        own_part(2 * full_width, HEAD_SIZE),
        own_part(2 * full_width + HEAD_SIZE, HEAD_SIZE),
    )
    return (outputs, d_inputs) + tuple(gradients)


def solution(mesh):
    return jax.shard_map(
        partial(body, dict(mesh.shape)),
        mesh=mesh,
        in_specs=(
            P("shard", "ctx", "tp"),
            P("shard", "tp"),
            P("shard", "tp"),
            P("shard", "tp"),
            P("tp", "shard"),
            P("shard", "tp"),
            P("shard", "tp"),
            P("tp", "shard"),
            P("shard"),
            P("shard"),
            P("shard"),
            P("shard"),
            P("shard", "ctx", "tp"),
        ),
        out_specs=(
            P("shard", "ctx", "tp"),
            P("shard", "ctx", "tp"),
            P(("shard", "ctx"), "tp"),
            P(("shard", "ctx"), "tp"),
            P(("shard", "ctx"), "tp"),
            P("tp", ("shard", "ctx")),
            P(("shard", "ctx"), "tp"),
            P(("shard", "ctx"), "tp"),
            P("tp", ("shard", "ctx")),
            P(("shard", "ctx")),
            P(("shard", "ctx")),
            P(("shard", "ctx")),
            P(("shard", "ctx")),
        ),
        check_vma=False,
    )
```
